32 devices in a mesh: dp: 4 (over z), tensor: 4 (over y, x), ctx: 2 (over core).
Axes of the slice: x: 2, y: 2, z: 4, core: 2. Of those that a mesh axis runs over, the one named last changes fastest.
Arguments:
- tokens: bfloat16 [4, 1024, 768], P('dp', ('ctx', 'tensor')), may hold values from -6 to 6
- lengths: int32 [4, 4], P('dp'), may hold values from 32 to 768, as said below
- norm1_gain: float32 [768], replicated, may hold values from 0.25 to 1.75
- norm1_shift: float32 [768], replicated, may hold values from -1.75 to 1.75
- qkv_weight: bfloat16 [768, 3, 768], P(None, None, 'tensor'), may hold values from -0.3125 to 0.3125
- query_bias: float32 [768], P('tensor'), may hold values from -3 to 3
- value_bias: float32 [768], P('tensor'), may hold values from -3 to 3
- output_projection_weight: bfloat16 [768, 768], P('tensor'), may hold values from -1.25 to 1.25
- out_bias: float32 [768], replicated, may hold values from -1.75 to 1.75
- norm2_gain: float32 [768], replicated, may hold values from 0.25 to 1.75
- norm2_shift: float32 [768], replicated, may hold values from -1.75 to 1.75
- up_projection_weight: bfloat16 [768, 3072], P(None, 'tensor'), may hold values from -0.21875 to 0.21875
- up_projection_bias: float32 [3072], P('tensor'), may hold values from -3 to 3
- down_projection_weight: bfloat16 [3072, 768], P('tensor'), may hold values from -0.15625 to 0.15625
- down_bias: float32 [768], replicated, may hold values from -1.75 to 1.75
- cotangent: bfloat16 [4, 1024, 768], P('dp', ('ctx', 'tensor')), may hold values from -6 to 6
Outputs:
- output: bfloat16 [4, 1024, 768], P('dp', ('ctx', 'tensor'))
- input_grad: bfloat16 [4, 1024, 768], P('dp', ('ctx', 'tensor'))
- norm1_gain_grad: float32 [768], replicated
- norm1_shift_grad: float32 [768], replicated
- qkv_weight_grad: float32 [768, 3, 768], P(None, None, 'tensor')
- query_bias_grad: float32 [768], P('tensor')
- value_bias_grad: float32 [768], P('tensor')
- out_weight_grad: float32 [768, 768], P('tensor')
- out_bias_grad: float32 [768], replicated
- norm2_gain_grad: float32 [768], replicated
- norm2_shift_grad: float32 [768], replicated
- up_weight_grad: float32 [768, 3072], P(None, 'tensor')
- up_bias_grad: float32 [3072], P('tensor')
- down_weight_grad: float32 [3072, 768], P('tensor')
- down_bias_grad: float32 [768], replicated
The draws below stay inside these ranges and needn't reach their ends.
Inputs may be any that keep to these rules, and one draw needn't show every extreme that they name: In each sequence the 4 documents lie in order and their lengths sum to 1024; the second document holds exactly 768 tokens and begins at a position from 64 to 128.
All inputs are finite; a program needn't handle non-finite values.
Results may differ from the reference program's by a relative error of at most 0.013.
The reference program's roundings to bfloat16 on the way count: a program that leaves them out, or rounds other values in their place, can miss the bound.
Values may be sent and summed in bfloat16 or wider, within the bound.
No kernel may reach another device: no remote copies, remote signals or barrier semaphores. Data moves between devices by JAX's collectives and lax.ppermute only.
A program may use at most 128 MiB of HBM per device.

```python
import jax
import jax.numpy as jnp
from jax import lax

D = 768
HEADS = 12
HEAD_DIM = 64
FF = 3072
LEN = 1024
SEQS = 4


def draw_lengths(key, part):
    key = jax.random.fold_in(key, 11)
    first_key, split_key = jax.random.split(key)
    long_doc = 3 * LEN // 4
    first_doc = jax.random.randint(first_key, (SEQS,), LEN // 16, LEN // 8 + 1)
    remain = LEN - long_doc - first_doc
    third_doc = jax.random.randint(split_key, (SEQS,), remain // 4, 3 * remain // 4 + 1)
    middle = jnp.full((SEQS,), long_doc, jnp.int32)
    return jnp.stack([first_doc, middle, third_doc, remain - third_doc], axis=-1).astype(jnp.int32)


def block_scale(rng, shape, shards, least, high):
    loudness = 1.0
    for position, parts in shards:
        heights = jax.random.uniform(jax.random.fold_in(jax.random.fold_in(rng, 6), position), (parts,), jnp.float32, least / len(shards), high / len(shards))
        loudness = loudness * jnp.repeat(jnp.exp(heights), shape[position] // parts).reshape((-1,) + (1,) * (len(shape) - 1 - position))
    return loudness


def noise(key, shape, deviation, bound, cuts=(), kind=jnp.bfloat16):
    array = jax.random.normal(key, shape, jnp.float32) * deviation
    if len(cuts) > 0:
        array = block_scale(key, shape, cuts, -0.22, 0.18) * array
    return jnp.clip(array, min=-bound, max=bound).astype(kind)


def setup_inputs(seed: int = 0) -> dict:
    key_list = jax.random.split(jax.random.key(seed), 17)
    tokens = noise(key_list[0], (SEQS, LEN, D), 1.0, 6.0, ((0, 4), (1, 8)))
    lengths = draw_lengths(jax.random.fold_in(key_list[16], 71), 0)
    norm1_gain = jnp.clip(1.0 + 0.15 * jax.random.normal(key_list[2], (D,), jnp.float32), 0.25, 1.75)
    norm1_shift = noise(key_list[3], (D,), 0.3, 1.75, (), jnp.float32)
    qkv_weight = noise(key_list[4], (D, 3, D), (D // 2) ** -0.5, 0.3125, ((2, 4),))
    query_bias = noise(key_list[5], (D,), 0.5, 3.0, ((0, 4),), jnp.float32)
    value_bias = noise(key_list[6], (D,), 0.5, 3.0, ((0, 4),), jnp.float32)
    output_projection_weight = noise(key_list[7], (D, D), (max(D // 32, 16)) ** -0.5, 1.25, ((0, 4),))
    out_bias = noise(key_list[8], (D,), 0.3, 1.75, (), jnp.float32)
    norm2_gain = jnp.clip(1.0 + 0.15 * jax.random.normal(key_list[9], (D,), jnp.float32), 0.25, 1.75)
    norm2_shift = noise(key_list[10], (D,), 0.3, 1.75, (), jnp.float32)
    up_projection_weight = noise(key_list[11], (D, FF), D ** -0.5, 0.21875, ((1, 4),))
    up_projection_bias = noise(key_list[12], (FF,), 0.5, 3.0, ((0, 4),), jnp.float32)
    down_projection_weight = noise(key_list[13], (FF, D), (FF // 2) ** -0.5, 0.15625, ((0, 4),))
    down_bias = noise(key_list[14], (D,), 0.3, 1.75, (), jnp.float32)
    cotangent = noise(key_list[15], (SEQS, LEN, D), 1.0, 6.0, ((0, 4), (1, 8)))
    return dict(tokens=tokens, lengths=lengths, norm1_gain=norm1_gain, norm1_shift=norm1_shift, qkv_weight=qkv_weight, query_bias=query_bias, value_bias=value_bias, output_projection_weight=output_projection_weight, out_bias=out_bias, norm2_gain=norm2_gain, norm2_shift=norm2_shift, up_projection_weight=up_projection_weight, up_projection_bias=up_projection_bias, down_projection_weight=down_projection_weight, down_bias=down_bias, cotangent=cotangent)


@jax.custom_vjp
def low(v):
    return lax.optimization_barrier(v.astype(jnp.bfloat16)).astype(jnp.float32)

@jax.custom_vjp
def reduced_backward(v):
    return v

def low_keep(v):
    return (low(v), None)

def low_pass(kept, grad):
    return (grad,)

def back_keep(v):
    return (v, None)

def back_low(kept, grad):
    return (low(grad),)
low.defvjp(low_keep, low_pass)
reduced_backward.defvjp(back_keep, back_low)
maximal_precision = lax.Precision.HIGHEST
norm_epsilon = 1e-05
masked_fill = -1e+30

def layer_norm(values, norm_gain, offset):
    center = values - lax.optimization_barrier(jnp.mean(values, axis=-1, keepdims=True))
    spread = lax.optimization_barrier(jnp.mean(center * center, axis=-1, keepdims=True))
    return center * lax.rsqrt(spread + norm_epsilon) * norm_gain + offset

def gelu_tanh(values):
    inner = 0.7978845608028654 * (values + 0.044715 * values * values * values)
    return 0.5 * values * (1.0 + jnp.tanh(inner))

def both_ways(values):
    return low(reduced_backward(values))

def segment_ids(lengths, length_all):
    bounds = jnp.cumsum(lengths, axis=-1).astype(jnp.int32)[..., :-1]
    places = jnp.arange(length_all, dtype=jnp.int32)
    return lax.optimization_barrier(jnp.sum((places[:, None] >= bounds[..., None, :]).astype(jnp.int32), axis=-1))

def attend_one(query_part, key_part, value_part, segment):
    dot_raw = jnp.einsum('qhe,khe->hqk', query_part, key_part, precision=maximal_precision)
    scores = reduced_backward(dot_raw * HEAD_DIM ** (-0.5))
    places = jnp.arange(LEN, dtype=jnp.int32)
    allowed = (places[None, :] <= places[:, None]) & (segment[None, :] == segment[:, None])
    masked = jnp.where(allowed[None], scores, masked_fill)
    row_max = lax.optimization_barrier(jnp.max(masked, axis=-1, keepdims=True))
    powers = jnp.exp(masked - row_max)
    weights = powers / lax.optimization_barrier(jnp.sum(powers, axis=-1, keepdims=True))
    return jnp.einsum('hqk,khe->qhe', low(weights), value_part, precision=maximal_precision)

def layer_forward(inputs, params, segments):
    gain_one, shift_one, query_key_value_matrix, query_b, value_b, output_matrix, output_bias_term, gain_two, shift_two, up_matrix, up_bias_term, down_matrix, down_bias_term = params
    group_size = inputs.shape[0]
    normalized_rows = low(layer_norm(inputs, gain_one, shift_one))
    projected_rows = jnp.einsum('zhy,yvi->zhvi', normalized_rows, query_key_value_matrix, precision=maximal_precision)
    head_shape = (group_size, LEN, HEADS, HEAD_DIM)
    queries = both_ways(projected_rows[:, :, 0] + query_b).reshape(head_shape)
    key_rows = both_ways(projected_rows[:, :, 1]).reshape(head_shape)
    value_rows = both_ways(projected_rows[:, :, 2] + value_b).reshape(head_shape)
    attend = jax.checkpoint(attend_one)

    def one_sequence(pieces):
        return attend(pieces[0], pieces[1], pieces[2], pieces[3])
    attention_mixture = lax.map(one_sequence, (queries, key_rows, value_rows, segments))
    attention_mixture = both_ways(attention_mixture.reshape(inputs.shape))
    branch_output = reduced_backward(jnp.einsum('tfb,bu->tfu', attention_mixture, output_matrix, precision=maximal_precision) + output_bias_term)
    hidden_state = inputs + branch_output
    second_normalized = low(layer_norm(hidden_state, gain_two, shift_two))
    up_projected = reduced_backward(jnp.einsum('mvg,gw->mvw', second_normalized, up_matrix, precision=maximal_precision) + up_bias_term)
    activated_rows = low(gelu_tanh(up_projected))
    return hidden_state + jnp.einsum('rcn,nu->rcu', activated_rows, down_matrix, precision=maximal_precision) + down_bias_term

def reference(tokens, lengths, norm1_gain, norm1_shift, qkv_weight, query_bias, value_bias, output_projection_weight, out_bias, norm2_gain, norm2_shift, up_projection_weight, up_projection_bias, down_projection_weight, down_bias, cotangent):
    params = tuple((piece.astype(jnp.float32) for piece in (norm1_gain, norm1_shift, qkv_weight, query_bias, value_bias, output_projection_weight, out_bias, norm2_gain, norm2_shift, up_projection_weight, up_projection_bias, down_projection_weight, down_bias)))
    group_size = max(1, min(SEQS, 4096 // LEN))
    while SEQS % group_size != 0:
        group_size = group_size - 1
    group_count = SEQS // group_size
    segments = segment_ids(lengths, LEN).reshape(group_count, group_size, LEN)
    inputs = tokens.astype(jnp.float32).reshape(group_count, group_size, LEN, D)
    starting_rows = cotangent.astype(jnp.float32).reshape(group_count, group_size, LEN, D)

    def one_group(totals, pieces):
        group_in, group_seed, group_segments = pieces

        def run_layer(values, weights):
            return layer_forward(values, weights, group_segments)
        result, pullback = jax.vjp(run_layer, group_in, params)
        grad_in, param_grads = pullback(group_seed)
        totals = jax.tree.map(jnp.add, totals, param_grads)
        return (totals, (result, grad_in))
    zero_grads = jax.tree.map(jnp.zeros_like, params)
    totals, (results, grads_in) = lax.scan(one_group, zero_grads, (inputs, starting_rows, segments))
    output = results.reshape(SEQS, LEN, D).astype(jnp.bfloat16)
    input_grad = grads_in.reshape(SEQS, LEN, D).astype(jnp.bfloat16)
    return (output, input_grad, totals[0], totals[1], totals[2], totals[3], totals[4], totals[5], totals[6], totals[7], totals[8], totals[9], totals[10], totals[11], totals[12])
```

```python
import jax
import jax.numpy as jnp
from jax import lax
from jax.sharding import PartitionSpec as P

HEAD_DIM = 64
EPS = 1e-05
MASKED = -1e30
BF16 = jnp.bfloat16
F32 = jnp.float32
SCALE = HEAD_DIM**-0.5


def dot(a, b, ca, cb):
    return lax.dot_general(a, b, (((ca,), (cb,)), ((), ())), preferred_element_type=F32)


def norm_parts(values):
    center = values - jnp.mean(values, axis=-1, keepdims=True)
    scale = lax.rsqrt(jnp.mean(center * center, axis=-1, keepdims=True) + EPS)
    return center * scale, scale


def norm_back(grad, gain, xhat, scale):
    g = grad * gain
    return scale * (
        g - jnp.mean(g, axis=-1, keepdims=True) - xhat * jnp.mean(g * xhat, axis=-1, keepdims=True)
    )


def gelu_tanh(values):
    inner = 0.7978845608028654 * (values + 0.044715 * values * values * values)
    return 0.5 * values * (1.0 + jnp.tanh(inner))


def xor_pairs(count, mask):
    return [(i, i ^ mask) for i in range(count)]


def pick(x, index):
    return lax.dynamic_index_in_dim(x, index, 0, keepdims=False)


def gather_rows(x, axis="tensor"):
    count = lax.axis_size(axis)
    me = lax.axis_index(axis)
    out = jnp.zeros((count,) + x.shape, x.dtype)
    out = lax.dynamic_update_slice_in_dim(out, x[None], me, 0)
    for r in range(1, count):
        got = lax.ppermute(x, axis, xor_pairs(count, r))
        out = lax.dynamic_update_slice_in_dim(out, got[None], me ^ r, 0)
    return out


def scatter_sum(x, axis="tensor"):
    count = lax.axis_size(axis)
    me = lax.axis_index(axis)
    low = x.astype(BF16)
    got = [
        lax.ppermute(pick(low, me ^ r), axis, xor_pairs(count, r)) for r in range(1, count)
    ]
    total = pick(x, me)
    for g in got:
        total = total + g.astype(F32)
    return total


def add_low(a, b):
    return (a.astype(F32) + b.astype(F32)).astype(BF16)


def sum_dp(x):
    count = lax.axis_size("dp")
    if count != 4:
        return lax.psum(x, "dp")
    bit = lax.axis_index("dp") & 1
    near, far = xor_pairs(4, 1), xor_pairs(4, 2)
    part = add_low(pick(x, bit), lax.ppermute(pick(x, 1 - bit), "dp", near))
    part = add_low(part, lax.ppermute(part, "dp", far))
    other = lax.ppermute(part, "dp", near)
    return jnp.where(bit == 0, jnp.stack([part, other]), jnp.stack([other, part]))


def sum_weights(x):
    rows, cols = x.shape
    me = lax.axis_index("ctx")
    pairs = xor_pairs(2, 1)
    x = x.reshape(2, rows // 2, cols)
    part = add_low(pick(x, me), lax.ppermute(pick(x, 1 - me), "ctx", pairs))
    part = sum_dp(part.reshape(2, rows // 4, cols)).reshape(rows // 2, cols)
    other = lax.ppermute(part, "ctx", pairs)
    out = jnp.where(me == 0, jnp.stack([part, other]), jnp.stack([other, part]))
    return out.reshape(rows, cols).astype(F32)


def sum_small(x, axis):
    count = lax.axis_size(axis)
    if count not in (2, 4):
        return lax.psum(x, axis)
    got = [lax.ppermute(x, axis, xor_pairs(count, r)) for r in range(1, count)]
    return sum(got, x)


def segment_ids(lengths, length_all):
    bounds = jnp.cumsum(lengths, axis=-1)[:-1]
    places = jnp.arange(length_all, dtype=jnp.int32)
    return jnp.sum((places[:, None] >= bounds[None, :]).astype(jnp.int32), axis=-1)


def per_device(
    tokens,
    lengths,
    norm1_gain,
    norm1_shift,
    qkv_weight,
    query_bias,
    value_bias,
    out_weight,
    out_bias,
    norm2_gain,
    norm2_shift,
    up_weight,
    up_bias,
    down_weight,
    down_bias,
    cotangent,
):
    tokens, cotangent, lengths = tokens[0], cotangent[0], lengths[0]
    own, width = tokens.shape
    ranks = lax.axis_size("tensor")
    half = own * ranks
    full = half * lax.axis_size("ctx")
    local = qkv_weight.shape[2]
    heads = local // HEAD_DIM
    rank = lax.axis_index("tensor")
    ctx = lax.axis_index("ctx")
    ctx_pairs = xor_pairs(2, 1)
    weight_t = jnp.transpose(qkv_weight, (1, 2, 0)).reshape(3 * local, width)

    rows = lax.all_gather(tokens, "tensor", axis=0, tiled=True).astype(F32)
    cot_rows = gather_rows(cotangent).reshape(half, width)
    half_weight = pick(out_weight.reshape(2, local // 2, width), ctx)
    half_weights = gather_rows(half_weight)
    other_weights = lax.ppermute(half_weights, "ctx", ctx_pairs)
    both = jnp.where(
        ctx == 0,
        jnp.stack([half_weights, other_weights], 1),
        jnp.stack([other_weights, half_weights], 1),
    )
    out_weight_all = both.reshape(ranks * local, width)

    xhat1, scale1 = norm_parts(rows)
    normed1 = (xhat1 * norm1_gain + norm1_shift).astype(BF16)
    qkv = dot(normed1, weight_t, 1, 1)
    queries = (qkv[:, :local] + query_bias).astype(BF16)
    keys = qkv[:, local : 2 * local].astype(BF16)
    values = (qkv[:, 2 * local :] + value_bias).astype(BF16)
    kv = jnp.concatenate([keys, values], 1)
    kv_other = lax.ppermute(kv, "ctx", ctx_pairs)
    kv_all = jnp.where(
        ctx == 0, jnp.concatenate([kv, kv_other], 0), jnp.concatenate([kv_other, kv], 0)
    )
    q_heads = queries.reshape(half, heads, HEAD_DIM)
    k_heads = kv_all[:, :local].reshape(full, heads, HEAD_DIM)
    v_heads = kv_all[:, local:].reshape(full, heads, HEAD_DIM)
    segment = segment_ids(lengths, full)
    q_place = ctx * half + jnp.arange(half, dtype=jnp.int32)
    k_place = jnp.arange(full, dtype=jnp.int32)
    q_segment = lax.dynamic_slice_in_dim(segment, ctx * half, half, 0)
    allowed = (k_place[None, :] <= q_place[:, None]) & (q_segment[:, None] == segment[None, :])

    def score_block():
        raw = jnp.einsum("qhe,khe->hqk", q_heads, k_heads, preferred_element_type=F32)
        return jnp.where(allowed[None], raw * SCALE, MASKED)

    scores = score_block()
    row_max = jnp.max(scores, axis=-1, keepdims=True)
    powers = jnp.exp(scores - row_max)
    row_total = jnp.sum(powers, axis=-1, keepdims=True)
    probs = powers / row_total
    log_total = row_max + jnp.log(row_total)
    mixture = (
        jnp.einsum("hqk,khe->qhe", probs.astype(BF16), v_heads, preferred_element_type=F32)
        .astype(BF16)
        .reshape(half, local)
    )
    mixtures = lax.all_gather(mixture, "tensor", axis=1, tiled=True)

    hidden = rows + dot(mixtures, out_weight_all, 1, 0) + out_bias
    xhat2, scale2 = norm_parts(hidden)
    normed2 = (xhat2 * norm2_gain + norm2_shift).astype(BF16)
    up = dot(normed2, up_weight, 1, 0) + up_bias
    active, gelu_pull = jax.vjp(gelu_tanh, up)
    active = active.astype(BF16)
    up_grad = gelu_pull(dot(cot_rows, down_weight, 1, 1))[0].astype(BF16)
    normed2_part = dot(up_grad, up_weight, 1, 1).reshape(ranks, own, width)
    normed2_grad = scatter_sum(normed2_part)

    down_part = dot(active, down_weight, 1, 0).reshape(ranks, own, width)
    down_grad = sum_weights(dot(active, cot_rows, 0, 0).astype(BF16))
    up_grad_weight = sum_weights(dot(normed2, up_grad, 0, 0).astype(BF16))

    own_hidden = pick(hidden.reshape(ranks, own, width), rank)
    own_xhat2 = pick(xhat2.reshape(ranks, own, width), rank)
    own_scale2 = pick(scale2.reshape(ranks, own, 1), rank)
    norm2_gain_part = jnp.sum(normed2_grad * own_xhat2, axis=0)
    norm2_shift_part = jnp.sum(normed2_grad, axis=0)
    hidden_grad = cotangent.astype(F32) + norm_back(normed2_grad, norm2_gain, own_xhat2, own_scale2)
    branch_grad = hidden_grad.astype(BF16)
    branch_rows = lax.all_gather(branch_grad, "tensor", axis=0, tiled=True)

    mixture_grad = dot(branch_rows, out_weight, 1, 1).astype(BF16).reshape(half, heads, HEAD_DIM)
    probs = jnp.exp(score_block() - log_total)
    prob_grad = jnp.einsum("qhe,khe->hqk", mixture_grad, v_heads, preferred_element_type=F32)
    value_part = jnp.einsum(
        "hqk,qhe->khe", probs.astype(BF16), mixture_grad, preferred_element_type=F32
    )
    center = jnp.sum(probs * prob_grad, axis=-1, keepdims=True)
    score_grad = (probs * (prob_grad - center)).astype(BF16)
    query_grad = jnp.einsum("hqk,khe->qhe", score_grad, k_heads, preferred_element_type=F32)
    query_grad = (query_grad * SCALE).astype(BF16).reshape(half, local)
    key_part = jnp.einsum("hqk,qhe->khe", score_grad, q_heads, preferred_element_type=F32) * SCALE
    kv_part = jnp.concatenate([key_part.reshape(full, local), value_part.reshape(full, local)], 1)
    kv_part = kv_part.reshape(2, half, 2 * local)
    kv_got = lax.ppermute(pick(kv_part, 1 - ctx).astype(BF16), "ctx", ctx_pairs)
    kv_grad = (pick(kv_part, ctx) + kv_got.astype(F32)).astype(BF16)
    grads = jnp.concatenate([query_grad, kv_grad], 1)
    qkv_grad = dot(grads, normed1, 0, 0).astype(BF16)
    out_grad = dot(mixture, branch_rows, 0, 0).astype(BF16)
    attn_grad = sum_weights(jnp.concatenate([qkv_grad, out_grad], 0))
    qkv_weight_grad = jnp.transpose(
        attn_grad[: 3 * local].reshape(3, local, width), (2, 0, 1)
    )
    out_weight_grad = attn_grad[3 * local :]

    normed1_part = dot(grads, weight_t, 1, 0)
    norm1_gain_part = jnp.sum(normed1_part * xhat1, axis=0)
    norm1_shift_part = jnp.sum(normed1_part, axis=0)
    normed1_grad = scatter_sum(normed1_part.reshape(ranks, own, width))
    own_xhat1 = pick(xhat1.reshape(ranks, own, width), rank)
    own_scale1 = pick(scale1.reshape(ranks, own, 1), rank)
    input_grad = hidden_grad + norm_back(normed1_grad, norm1_gain, own_xhat1, own_scale1)
    output = own_hidden + scatter_sum(down_part) + down_bias

    by_rank = sum_small(
        jnp.stack([norm1_gain_part, norm1_shift_part, norm2_gain_part, norm2_shift_part]), "tensor"
    )
    grads_sum = jnp.sum(grads.astype(F32), axis=0)
    bias_row = jnp.concatenate([grads_sum[:local], grads_sum[2 * local :]])
    bias_row = jnp.pad(bias_row, (0, width - 2 * local))
    up_bias_part = jnp.sum(up_grad.astype(F32), axis=0)
    small = jnp.concatenate(
        [
            by_rank,
            jnp.stack(
                [
                    jnp.sum(branch_rows.astype(F32), axis=0),
                    jnp.sum(cot_rows.astype(F32), axis=0),
                    up_bias_part,
                    bias_row,
                ]
            ),
        ],
        0,
    )
    small = sum_small(sum_small(small, "ctx"), "dp")
    return (
        output.astype(BF16)[None],
        input_grad.astype(BF16)[None],
        small[0],
        small[1],
        qkv_weight_grad,
        small[7, :local],
        small[7, local : 2 * local],
        out_weight_grad,
        small[4],
        small[2],
        small[3],
        up_grad_weight,
        small[6],
        down_grad,
        small[5],
    )


def solution(mesh):
    row_spec = P("dp", ("ctx", "tensor"), None)
    return jax.shard_map(
        per_device,
        mesh=mesh,
        in_specs=(
            row_spec,
            P("dp", None),
            P(),
            P(),
            P(None, None, "tensor"),
            P("tensor"),
            P("tensor"),
            P("tensor", None),
            P(),
            P(),
            P(),
            P(None, "tensor"),
            P("tensor"),
            P("tensor", None),
            P(),
            row_spec,
        ),
        out_specs=(
            row_spec,
            row_spec,
            P(),
            P(),
            P(None, None, "tensor"),
            P("tensor"),
            P("tensor"),
            P("tensor", None),
            P(),
            P(),
            P(),
            P(None, "tensor"),
            P("tensor"),
            P("tensor", None),
            P(),
        ),
        check_vma=False,
    )
```

```python
import functools

import jax
import jax.numpy as jnp
from jax import lax
from jax.experimental import pallas as pl
from jax.experimental.pallas import tpu as pltpu
from jax.sharding import PartitionSpec as P

HEAD_DIM = 64
EPS = 1e-05
MASKED = -1e30
BF16 = jnp.bfloat16
F32 = jnp.float32
SCALE = HEAD_DIM**-0.5
LOG2_SCALE = SCALE * 1.4426950408889634
LONG_START_MAX = 128
LONG_END_MIN = 64 + 768
LONG_END_MAX = 128 + 768
MIB = 1024 * 1024


def dot(a, b, ca, cb):
    return lax.dot_general(a, b, (((ca,), (cb,)), ((), ())), preferred_element_type=F32)


def norm_parts(values):
    center = values - jnp.mean(values, axis=-1, keepdims=True)
    scale = lax.rsqrt(jnp.mean(center * center, axis=-1, keepdims=True) + EPS)
    return center * scale, scale


def norm_back(grad, gain, xhat, scale):
    g = grad * gain
    return scale * (
        g - jnp.mean(g, axis=-1, keepdims=True) - xhat * jnp.mean(g * xhat, axis=-1, keepdims=True)
    )


def xor_pairs(count, mask):
    return [(i, i ^ mask) for i in range(count)]


def pick(x, index):
    return lax.dynamic_index_in_dim(x, index, 0, keepdims=False)


def after(x, *deps):
    return lax.optimization_barrier((x,) + deps)[0]


def rows_at(index, size):
    return pl.ds(pl.multiple_of(index * size, size), size)


def call(kernel, out_shape, args, vmem=16, scratch=(), smem=0):
    spaces = [pltpu.SMEM] * smem + [pltpu.VMEM] * (len(args) - smem)
    return pl.pallas_call(
        kernel,
        out_shape=out_shape,
        in_specs=[pl.BlockSpec(memory_space=s) for s in spaces],
        out_specs=[pl.BlockSpec(memory_space=pltpu.VMEM)] * len(out_shape),
        scratch_shapes=list(scratch),
        compiler_params=pltpu.CompilerParams(vmem_limit_bytes=vmem * MIB),
    )(*args)


def vec(ref):
    return ref[...].reshape(1, ref.shape[0])


def shape(dims, dtype):
    return jax.ShapeDtypeStruct(dims, dtype)


def qkv_kernel(
    meta_ref, x0, x1, x2, x3, gain_ref, shift_ref, w_ref, qb_ref, vb_ref, rows_ref, normed_ref, q_ref, kv_ref
):
    local = q_ref.shape[1]
    own = x0.shape[0]
    rank = meta_ref[0]
    gain, shift = vec(gain_ref), vec(shift_ref)
    for r, x in enumerate((x0, x1, x2, x3)):
        at = rows_at(rank ^ r, own)
        rows_ref[at] = x[...]
        xhat, _ = norm_parts(x[...].astype(F32))
        normed_ref[at] = (xhat * gain + shift).astype(BF16)
    normed = normed_ref[...]
    q_ref[...] = (dot(normed, w_ref[:local], 1, 1) + vec(qb_ref)).astype(BF16)
    kv_ref[:, :local] = dot(normed, w_ref[local : 2 * local], 1, 1).astype(BF16)
    kv_ref[:, local:] = (dot(normed, w_ref[2 * local :], 1, 1) + vec(vb_ref)).astype(BF16)


def blocks_of(ctx, half, size):
    out = []
    for i in range(half // size):
        first = ctx * half + i * size
        low = LONG_END_MIN // 128 * 128 if first >= LONG_END_MAX else 0
        out.append((i * size, first, low, first + size))
    return out


def allowed_of(meta_ref, first, low, end, size):
    query = first + lax.broadcasted_iota(jnp.int32, (1, size), 1)
    start = jnp.zeros_like(query)
    bound = jnp.int32(0)
    for j in range(3):
        bound = bound + meta_ref[2 + j]
        start = jnp.where(query >= bound, bound, start)
    key = low + lax.broadcasted_iota(jnp.int32, (end - low, size), 0)
    return (key >= start) & (key <= query)


def head_mask(head, width):
    lane = lax.broadcasted_iota(jnp.int32, (1, width), 1)
    inside = (lane >= head * HEAD_DIM) & (lane < (head + 1) * HEAD_DIM)
    return jnp.where(inside, 1.0, 0.0).astype(BF16)


def attend_body(ctx, size, meta_ref, q_ref, k_ref, vt_ref, mix_ref, lse_ref):
    half, local = q_ref.shape
    for at, first, low, end in blocks_of(ctx, half, size):
        allowed = allowed_of(meta_ref, first, low, end, size)
        cols = slice(at, at + size)
        for h in range(local // HEAD_DIM):
            feats = slice(h * HEAD_DIM, (h + 1) * HEAD_DIM)
            q = q_ref[cols] * head_mask(h, local)
            s = dot(k_ref[low:end], q, 1, 1)
            s = jnp.where(allowed, s * LOG2_SCALE, MASKED)
            top = jnp.max(s, axis=0, keepdims=True)
            p = jnp.exp2(s - top)
            total = jnp.sum(p, axis=0, keepdims=True)
            p = p * (1.0 / total)
            lse_ref[h : h + 1, cols] = top + jnp.log2(total)
            mix = dot(vt_ref[feats, low:end], p.astype(BF16), 1, 0)
            mix_ref[feats, cols] = mix.astype(BF16)


def attend_kernel(size, meta_ref, q_ref, kv_ref, mix_ref, lse_ref, k_all, vt_all):
    half, local = q_ref.shape
    ctx = meta_ref[1]

    @pl.when(ctx == 0)
    def _():
        k_all[:half] = kv_ref[:half, :local]
        kvt = kv_ref[:half].T
        vt_all[:, :half] = kvt[local:]
        attend_body(0, size, meta_ref, q_ref, k_all, vt_all, mix_ref, lse_ref)

    @pl.when(ctx != 0)
    def _():
        k_all[...] = kv_ref[:, :local]
        kvt = kv_ref[...].T
        vt_all[...] = kvt[local:]
        attend_body(1, size, meta_ref, q_ref, k_all, vt_all, mix_ref, lse_ref)


def back_body(ctx, size, meta_ref, q_ref, d_ref, lse_ref, k_ref, kt_ref, v_ref, dq_ref, dk, dv, p_all, s_all):
    half, local = q_ref.shape
    heads = local // HEAD_DIM
    for at, first, low, end in blocks_of(ctx, half, size):
        allowed = allowed_of(meta_ref, first, low, end, size)
        cols = slice(at, at + size)
        keys = slice(low, end)
        qs, ds = [], []
        for h in range(heads):
            feats = slice(h * HEAD_DIM, (h + 1) * HEAD_DIM)
            mask = head_mask(h, local)
            q = q_ref[cols] * mask
            d = d_ref[cols] * mask
            qs.append(q)
            ds.append(d)
            s = dot(k_ref[keys], q, 1, 1)
            p = jnp.exp2(jnp.where(allowed, s * LOG2_SCALE - lse_ref[h : h + 1, cols], MASKED))
            dp = dot(v_ref[keys], d, 1, 1)
            center = jnp.sum(p * dp, axis=0, keepdims=True)
            score = (p * (dp - center)).astype(BF16)
            lanes = slice(h * size, (h + 1) * size)
            p_all[keys, lanes] = p.astype(BF16)
            s_all[keys, lanes] = score
            dq_ref[feats, cols] = (dot(kt_ref[feats, keys], score, 1, 0) * SCALE).astype(BF16)
        dk[keys] += dot(s_all[keys], jnp.concatenate(qs, 0), 1, 0)
        dv[keys] += dot(p_all[keys], jnp.concatenate(ds, 0), 1, 0)


def back_kernel(
    size, meta_ref, q_ref, kv_ref, lse_ref, b0, b1, b2, b3, w_ref,
    dq_ref, keep_ref, send_ref, rows_ref, k_all, kt_all, v_all, d_all, dk, dv, p_all, s_all,
):
    half, local = q_ref.shape
    own = b0.shape[0]
    rank, ctx = meta_ref[0], meta_ref[1]
    for r, b in enumerate((b0, b1, b2, b3)):
        rows_ref[rows_at(rank ^ r, own)] = b[...]
    d_all[...] = dot(rows_ref[...], w_ref[...], 1, 1).astype(BF16)
    rest = (dq_ref, dk, dv, p_all, s_all)

    @pl.when(ctx == 0)
    def _():
        k_all[:half] = kv_ref[:half, :local]
        v_all[:half] = kv_ref[:half, local:]
        kt_all[:, :half] = k_all[:half].T
        dk[:half] = jnp.zeros((half, local), F32)
        dv[:half] = jnp.zeros((half, local), F32)
        back_body(0, size, meta_ref, q_ref, d_all, lse_ref, k_all, kt_all, v_all, *rest)
        keep_ref[:, :local] = dk[:half] * SCALE
        keep_ref[:, local:] = dv[:half]
        send_ref[...] = jnp.zeros(send_ref.shape, BF16)

    @pl.when(ctx != 0)
    def _():
        k_all[...] = kv_ref[:, :local]
        v_all[...] = kv_ref[:, local:]
        kt_all[...] = k_all[...].T
        dk[...] = jnp.zeros(dk.shape, F32)
        dv[...] = jnp.zeros(dv.shape, F32)
        back_body(1, size, meta_ref, q_ref, d_all, lse_ref, k_all, kt_all, v_all, *rest)
        send_ref[:, :local] = (dk[:half] * SCALE).astype(BF16)
        send_ref[:, local:] = dv[:half].astype(BF16)
        keep_ref[:, :local] = dk[half:] * SCALE
        keep_ref[:, local:] = dv[half:]


def ff_kernel(
    meta_ref, m0, m1, m2, m3, x_ref, w_ref, wa_ref, wb_ref, ob_ref, gain_ref, shift_ref, up_ref, ub_ref, down_ref, c0, c1, c2, c3,
    normed_ref, active_ref, upg_ref, cot_ref, hidden_ref, s0, s1, s2, s3, ub_out, db_out, w_all, mix_all, part,
):
    own = c0.shape[0]
    half = x_ref.shape[0]
    local = w_ref.shape[0]
    rank, ctx = meta_ref[0], meta_ref[1]
    piece = local // 2
    w_all[:local] = w_ref[...]
    for r in range(wa_ref.shape[0] // piece):
        w_all[rows_at(2 * (r + 1) + ctx, piece)] = wa_ref[r * piece : (r + 1) * piece]
        w_all[rows_at(2 * (r + 1) + 1 - ctx, piece)] = wb_ref[rows_at((1 - ctx) * 3 + r, piece)]
    for r, m in enumerate((m0, m1, m2, m3)):
        mix_all[r * local : (r + 1) * local] = m[...]
    for r, c in enumerate((c0, c1, c2, c3)):
        cot_ref[rows_at(rank ^ r, own)] = c[...]
    chunk = 256
    ob, gain, shift, ub = vec(ob_ref), vec(gain_ref), vec(shift_ref), vec(ub_ref)
    ub_total = jnp.zeros(ub_out.shape, F32)
    db_total = jnp.zeros(db_out.shape, F32)
    for i in range(half // chunk):
        at = slice(i * chunk, (i + 1) * chunk)
        hidden = dot(mix_all[:, at], w_all[...], 0, 0) + x_ref[at].astype(F32) + ob
        part[at] = hidden
        xhat, _ = norm_parts(hidden)
        normed_ref[at] = (xhat * gain + shift).astype(BF16)
    hidden_ref[...] = part[rows_at(rank, own)]
    for i in range(half // chunk):
        at = slice(i * chunk, (i + 1) * chunk)
        v = dot(normed_ref[at], up_ref[...], 1, 0) + ub
        d = dot(cot_ref[at], down_ref[...], 1, 1)
        square = v * v
        t = jnp.tanh(0.7978845608028654 * v * (1.0 + 0.044715 * square))
        active_ref[at] = (0.5 * v * (1.0 + t)).astype(BF16)
        slope = 0.5 * (1.0 + t) + (0.5 * 0.7978845608028654) * v * (1.0 - t * t) * (
            1.0 + 3.0 * 0.044715 * square
        )
        g = (d * slope).astype(BF16)
        upg_ref[at] = g
        ub_total += jnp.sum(g.astype(F32), axis=0, keepdims=True)
        db_total += jnp.sum(cot_ref[at].astype(F32), axis=0, keepdims=True)
        part[at] = dot(g, up_ref[...], 1, 1)
    ub_out[...] = ub_total
    db_out[...] = db_total
    s0[...] = part[rows_at(rank, own)]
    for r, s in enumerate((s1, s2, s3), 1):
        s[...] = part[rows_at(rank ^ r, own)].astype(BF16)


def quarters_out(meta_ref, total, quarters):
    ctx, bit = meta_ref[1], meta_ref[6]
    size = quarters[0].shape[0]
    own, near, far_near, far_own = quarters
    own[...] = total[rows_at(2 * ctx + bit, size)]
    near[...] = total[rows_at(2 * ctx + 1 - bit, size)]
    far_near[...] = total[rows_at(3 - 2 * ctx - bit, size)]
    far_own[...] = total[rows_at(2 - 2 * ctx + bit, size)]


def weight_grad_kernel(meta_ref, a_ref, b_ref, *refs):
    total = refs[4]
    total[...] = dot(a_ref[...], b_ref[...], 0, 0).astype(BF16)
    quarters_out(meta_ref, total, refs[:4])


def out_part_kernel(meta_ref, active_ref, down_ref, s0, s1, s2, s3, part):
    rank = meta_ref[0]
    own = s0.shape[0]
    part[...] = dot(active_ref[...], down_ref[...], 1, 0)
    s0[...] = part[rows_at(rank, own)]
    for r, s in enumerate((s1, s2, s3), 1):
        s[...] = part[rows_at(rank ^ r, own)].astype(BF16)


def sum4(refs):
    total = refs[0][...]
    for ref in refs[1:]:
        total = total + ref[...].astype(F32)
    return total


def norm2_back_kernel(s0, g1, g2, g3, hidden_ref, cot_ref, gain_ref, grad_ref, low_ref, small_ref):
    grad = sum4((s0, g1, g2, g3))
    xhat, scale = norm_parts(hidden_ref[...])
    hidden_grad = cot_ref[...].astype(F32) + norm_back(grad, vec(gain_ref), xhat, scale)
    grad_ref[...] = hidden_grad
    low_ref[...] = hidden_grad.astype(BF16)
    small_ref[0:1] = jnp.sum(grad * xhat, axis=0, keepdims=True)
    small_ref[1:2] = jnp.sum(grad, axis=0, keepdims=True)


def q_back_kernel(
    meta_ref, dq_ref, normed_ref, mix_ref, rows_ref, w_ref, t0, t1, t2, t3, part_ref, qb_ref, ob_ref, total
):
    local = dq_ref.shape[0]
    dq = dq_ref[...]
    total[:local] = dot(dq, normed_ref[...], 1, 0).astype(BF16)
    total[local:] = dot(mix_ref[...], rows_ref[...], 1, 0).astype(BF16)
    quarters_out(meta_ref, total, (t0, t1, t2, t3))
    part_ref[...] = dot(dq, w_ref[:local], 0, 0)
    qb_ref[...] = dot(jnp.ones((8, dq.shape[1]), BF16), dq, 1, 1)[0:1]
    ob_ref[...] = jnp.sum(rows_ref[...].astype(F32), axis=0, keepdims=True)


def kv_back_kernel(
    meta_ref, keep_kv, got_kv, normed_ref, w_ref, x_ref, norm2_ref, qpart_ref,
    t0, t1, t2, t3, s0, s1, s2, s3, norm_ref, vb_ref, total, part,
):
    rank, ctx = meta_ref[0], meta_ref[1]
    own, width = s0.shape
    half, local = keep_kv.shape[0], keep_kv.shape[1] // 2
    normed = normed_ref[...]
    dkv = (keep_kv[...] + got_kv[rows_at(1 - ctx, half)].astype(F32)).astype(BF16)
    total[...] = dot(dkv, normed, 0, 0).astype(BF16)
    quarters_out(meta_ref, total, (t0, t1, t2, t3))
    part[...] = qpart_ref[...] + dot(dkv, w_ref[local:], 1, 0)
    gain_total = jnp.zeros((1, width), F32)
    shift_total = jnp.zeros((1, width), F32)
    chunk = 128
    for c in range(half // chunk):
        at = slice(c * chunk, (c + 1) * chunk)
        xhat, _ = norm_parts(x_ref[at].astype(F32))
        gain_total += jnp.sum(part[at] * xhat, axis=0, keepdims=True)
        shift_total += jnp.sum(part[at], axis=0, keepdims=True)
    norms = jnp.concatenate(
        [gain_total, shift_total, norm2_ref[...], jnp.zeros((4, width), F32)], 0
    )
    norm_ref[...] = norms
    high = norms.astype(BF16)
    tail = jnp.concatenate([high.astype(F32), norms - high.astype(F32)], 0).astype(BF16)
    s0[...] = part[rows_at(rank, own)]
    for r, s in enumerate((s1, s2, s3), 1):
        s[:own] = part[rows_at(rank ^ r, own)].astype(BF16)
        s[own:] = tail
    vb_ref[...] = jnp.sum(dkv.astype(F32), axis=0, keepdims=True)[:, local:]


def norm1_back_kernel(
    s0, g1, g2, g3, x_ref, gain_ref, hidden_ref, norm_ref, ob_ref, db_ref, ub_ref, qb_ref, vb_ref, out_ref, small_ref
):
    own = s0.shape[0]
    grad = s0[...]
    norms = norm_ref[...]
    for g in (g1, g2, g3):
        grad = grad + g[:own].astype(F32)
        tail = g[own:].astype(F32)
        norms = norms + (tail[:8] + tail[8:])
    xhat, scale = norm_parts(x_ref[...].astype(F32))
    out = hidden_ref[...] + norm_back(grad, vec(gain_ref), xhat, scale)
    out_ref[...] = out.astype(BF16)
    local = qb_ref.shape[1]
    small_ref[0:4] = norms[:4]
    small_ref[4:5] = ob_ref[...]
    small_ref[5:6] = db_ref[...]
    small_ref[6:7] = ub_ref[...]
    small_ref[7:8] = jnp.zeros_like(ob_ref)
    small_ref[7:8, :local] = qb_ref[...]
    lanes = small_ref.shape[1] // 2
    small_ref[7:8, lanes : lanes + local] = vb_ref[...]


def output_kernel(s0, g1, g2, g3, hidden_ref, bias_ref, out_ref):
    out_ref[...] = (hidden_ref[...] + sum4((s0, g1, g2, g3)) + vec(bias_ref)).astype(BF16)


def place(meta_ref, own_ref, other_ref, own_all, other_all, out_ref):
    ctx, bit = meta_ref[1], meta_ref[6]
    size = own_ref.shape[0]
    out_ref[rows_at(2 * ctx + bit, size)] = own_ref[...].astype(F32)
    out_ref[rows_at(2 * ctx + 1 - bit, size)] = other_ref[...].astype(F32)
    peer = rows_at(1 - ctx, size)
    out_ref[rows_at(2 - 2 * ctx + bit, size)] = own_all[peer].astype(F32)
    out_ref[rows_at(3 - 2 * ctx - bit, size)] = other_all[peer].astype(F32)


def whole_kernel(meta_ref, own_ref, other_ref, own_all, other_all, out_ref):
    place(meta_ref, own_ref, other_ref, own_all, other_all, out_ref)


def attn_whole_kernel(meta_ref, *refs):
    qkv_out, out_out, total = refs[8:]
    local = out_out.shape[0]
    place(meta_ref, *refs[:4], total)
    qkv_out[:local] = total[:local]
    out_out[...] = total[local:]
    place(meta_ref, *refs[4:8], total)
    qkv_out[local:] = total[...]


def small_kernel(a, b, c, d, *outs):
    total = a[...] + b[...] + c[...] + d[...]
    for i, out in enumerate(outs[:7]):
        out[...] = total[i]
    local = outs[7].shape[0]
    lanes = total.shape[1] // 2
    outs[7][...] = total[7, :local]
    outs[8][...] = total[7, lanes : lanes + local]


def to_peers(blocks):
    return [
        lax.ppermute(b, "tensor", xor_pairs(lax.axis_size("tensor"), r))
        for r, b in enumerate(blocks, 1)
    ]


NEAR, FAR = xor_pairs(4, 1), xor_pairs(4, 2)


def peer_add_kernel(meta_ref, a_ref, pair_ref, out_ref):
    size = a_ref.shape[0]
    got = pair_ref[rows_at(1 - meta_ref[1], size)].astype(F32)
    out_ref[...] = (a_ref[...].astype(F32) + got).astype(BF16)


def peer_add2_kernel(meta_ref, a_ref, pair_ref, b_ref, out_ref):
    size = a_ref.shape[0]
    got = pair_ref[rows_at(1 - meta_ref[1], size)].astype(F32)
    out_ref[...] = (a_ref[...].astype(F32) + got + b_ref[...].astype(F32)).astype(BF16)


def add_kernel(a_ref, b_ref, out_ref):
    out_ref[...] = (a_ref[...].astype(F32) + b_ref[...].astype(F32)).astype(BF16)


class Order:
    def __init__(self):
        self.last = None

    def first(self, x):
        return x if self.last is None else after(x, self.last)

    def call(self, kernel, out_shape, args, at=-1, **kw):
        args = list(args)
        args[at] = self.first(args[at])
        out = call(kernel, out_shape, args, **kw)
        self.last = out[0]
        return out

    def pair(self, x):
        self.last = lax.all_gather(self.first(x), "ctx", axis=0, tiled=True)
        return self.last


class WeightSum:
    def __init__(self, order, meta, quarters):
        self.order, self.meta = order, meta
        self.own, self.near, self.far_near, self.far_own = quarters
        self.shape = [shape(self.own.shape, BF16)]
        self.short = lax.axis_size("dp") == 4

    def one(self):
        got = self.order.pair(self.far_near)
        (send,) = self.order.call(
            peer_add_kernel, self.shape, [self.meta, self.near, got], smem=1
        )
        self.got = lax.ppermute(send, "dp", NEAR) if self.short else lax.psum(send, "dp")

    def two(self):
        self.pairs = self.order.pair(self.far_own)

    def three(self):
        other = self.got if self.short else jnp.zeros_like(self.got)
        (self.own,) = self.order.call(
            peer_add2_kernel, self.shape, [self.meta, self.own, self.pairs, other], smem=1
        )
        if self.short:
            self.got = lax.ppermute(self.own, "dp", FAR)
        else:
            self.own = lax.psum(self.own, "dp")

    def four(self):
        if self.short:
            (self.own,) = self.order.call(add_kernel, self.shape, [self.own, self.got])
            self.got = lax.ppermute(self.own, "dp", NEAR)

    def five(self):
        self.own_all = self.order.pair(self.own)

    def six(self):
        self.got_all = self.order.pair(self.got)

    def parts(self):
        return [self.own, self.got, self.own_all, self.got_all]

    def whole(self):
        rows, cols = self.own.shape
        return self.order.call(
            whole_kernel, [shape((4 * rows, cols), F32)], [self.meta, *self.parts()], smem=1
        )[0]


def per_device(
    tokens,
    lengths,
    norm1_gain,
    norm1_shift,
    qkv_weight,
    query_bias,
    value_bias,
    out_weight,
    out_bias,
    norm2_gain,
    norm2_shift,
    up_weight,
    up_bias,
    down_weight,
    down_bias,
    cotangent,
):
    tokens, cotangent = tokens[0], cotangent[0]
    own, width = tokens.shape
    ranks = lax.axis_size("tensor")
    half = own * ranks
    full = half * lax.axis_size("ctx")
    local = qkv_weight.shape[2]
    hidden_units = up_weight.shape[1]
    rank = lax.axis_index("tensor")
    ctx = lax.axis_index("ctx")
    bit = lax.axis_index("dp") & 1
    meta = jnp.concatenate(
        [jnp.stack([rank, ctx]).astype(jnp.int32), lengths[0], bit.astype(jnp.int32)[None]]
    )
    weight_t = jnp.transpose(qkv_weight, (1, 2, 0)).reshape(3 * local, width)
    size = 128
    block = shape((own, width), F32)
    block_low = shape((own, width), BF16)
    row_out = shape((1, width), F32)

    def quarters(rows_all, cols):
        return [shape((rows_all // 4, cols), BF16)] * 4

    order = Order()
    xs = to_peers([tokens] * 3)
    out_half = pick(out_weight.reshape(2, local // 2, width), ctx)
    out_halves = to_peers([out_half] * 3)
    rows, normed1, q, kv = order.call(
        qkv_kernel,
        [shape((half, width), BF16)] * 2
        + [shape((half, local), BF16), shape((half, 2 * local), BF16)],
        [meta, tokens, *xs, norm1_gain, norm1_shift, weight_t, query_bias, value_bias],
        smem=1,
    )
    cots = to_peers([after(cotangent, kv)] * 3)
    kv_all = order.pair(kv)
    mix, lse = order.call(
        functools.partial(attend_kernel, size),
        [shape((local, half), BF16), shape((8, half), F32)],
        [meta, q, kv_all],
        smem=1,
        scratch=[pltpu.VMEM((full, local), BF16), pltpu.VMEM((local, full), BF16)],
    )
    mixes = to_peers([mix] * 3)
    out_half = jnp.concatenate([after(out_halves[0], mix, *cots), *out_halves[1:]], 0)
    out_both = order.pair(out_half)
    (normed2, active, up_grad, cot_rows, hidden, *normed2_parts, up_bias_part, down_bias_part) = order.call(
        ff_kernel,
        [
            shape((half, width), BF16),
            shape((half, hidden_units), BF16),
            shape((half, hidden_units), BF16),
            shape((half, width), BF16),
            block,
            block,
            block_low,
            block_low,
            block_low,
            shape((1, hidden_units), F32),
            row_out,
        ],
        [meta, mix, *mixes, rows, out_weight, out_half, out_both, out_bias, norm2_gain, norm2_shift]
        + [up_weight, up_bias, down_weight, cotangent, *cots],
        smem=1,
        vmem=28,
        scratch=[
            pltpu.VMEM((ranks * local, width), BF16),
            pltpu.VMEM((ranks * local, half), BF16),
            pltpu.VMEM((half, width), F32),
        ],
    )
    normed2_got = to_peers(normed2_parts[1:])

    def weight_grad(a, b):
        rows_all, cols = a.shape[1], b.shape[1]
        out = order.call(
            weight_grad_kernel,
            quarters(rows_all, cols),
            [meta, a, b],
            smem=1,
            scratch=[pltpu.VMEM((rows_all, cols), BF16)],
        )
        return WeightSum(order, meta, out)

    down_sum = weight_grad(active, cot_rows)
    down_sum.one()
    up_sum = weight_grad(normed2, up_grad)
    hidden_grad, branch_grad, norm2_part = order.call(
        norm2_back_kernel,
        [block, block_low, shape((2, width), F32)],
        [normed2_parts[0], *normed2_got, hidden, cotangent, norm2_gain],
        at=0,
    )
    branches = to_peers([branch_grad] * 3)
    down_sum.two()
    up_sum.one()
    out_parts = order.call(
        out_part_kernel,
        [block, block_low, block_low, block_low],
        [meta, active, down_weight],
        at=1,
        smem=1,
        scratch=[pltpu.VMEM((half, width), F32)],
    )
    down_sum.three()
    up_sum.two()
    dq, kv_keep, kv_send, branch_rows = order.call(
        functools.partial(back_kernel, size),
        [
            shape((local, half), BF16),
            shape((half, 2 * local), F32),
            shape((half, 2 * local), BF16),
            shape((half, width), BF16),
        ],
        [meta, q, kv_all, lse, branch_grad, *branches, out_weight],
        at=1,
        smem=1,
        vmem=24,
        scratch=[
            pltpu.VMEM((full, local), BF16),
            pltpu.VMEM((local, full), BF16),
            pltpu.VMEM((full, local), BF16),
            pltpu.VMEM((half, local), BF16),
            pltpu.VMEM((full, local), F32),
            pltpu.VMEM((full, local), F32),
            pltpu.VMEM((full, local // HEAD_DIM * size), BF16),
            pltpu.VMEM((full, local // HEAD_DIM * size), BF16),
        ],
    )
    up_sum.three()
    kv_got = order.pair(kv_send)
    *qo_quarters, q_part, q_bias_part, out_bias_part = order.call(
        q_back_kernel,
        quarters(2 * local, width) + [shape((half, width), F32), shape((1, local), F32), row_out],
        [meta, dq, normed1, mix, branch_rows, weight_t],
        at=1,
        smem=1,
        scratch=[pltpu.VMEM((2 * local, width), BF16)],
    )
    qo_sum = WeightSum(order, meta, qo_quarters)
    qo_sum.one()
    tail_low = shape((own + 16, width), BF16)
    *kv_quarters, n0, n1, n2, n3, norm_part, v_bias_part = order.call(
        kv_back_kernel,
        quarters(2 * local, width)
        + [block, tail_low, tail_low, tail_low, shape((8, width), F32), shape((1, local), F32)],
        [meta, kv_keep, kv_got, normed1, weight_t, rows, norm2_part, q_part],
        smem=1,
        scratch=[pltpu.VMEM((2 * local, width), BF16), pltpu.VMEM((half, width), F32)],
    )
    normed1_got = to_peers([n1, n2, n3])
    kv_sum = WeightSum(order, meta, kv_quarters)
    kv_sum.one()
    down_sum.four()
    qo_sum.two()
    down_sum.five()
    qo_sum.three()
    input_grad, small = order.call(
        norm1_back_kernel,
        [block_low, shape((8, width), F32)],
        [n0, *normed1_got, tokens, norm1_gain, hidden_grad, norm_part, out_bias_part]
        + [down_bias_part, up_bias_part, q_bias_part, v_bias_part],
        at=0,
    )
    out_got = to_peers([after(b, input_grad) for b in out_parts[1:]])
    kv_sum.two()
    kv_sum.three()
    small = order.pair(small)
    small = small[:8] + small[8:]
    down_sum.six()
    up_sum.four()
    up_sum.five()
    if lax.axis_size("dp") == 4:
        smalls = [small] + [lax.ppermute(small, "dp", xor_pairs(4, r)) for r in (1, 2, 3)]
    else:
        small = lax.psum(small, "dp")
        smalls = [small] + [jnp.zeros_like(small)] * 3
    (output,) = order.call(
        output_kernel, [block_low], [out_parts[0], *out_got, hidden, down_bias], at=0
    )
    down_grad = down_sum.whole()
    qo_sum.four()
    qo_sum.five()
    kv_sum.four()
    kv_sum.five()
    up_sum.six()
    up_weight_grad = up_sum.whole()
    outs = order.call(
        small_kernel,
        [shape((width,), F32)] * 7 + [shape((local,), F32)] * 2,
        smalls,
        at=0,
    )
    qo_sum.six()
    kv_sum.six()
    attn_grad, out_weight_grad = order.call(
        attn_whole_kernel,
        [shape((3 * local, width), F32), shape((local, width), F32)],
        [meta, *qo_sum.parts(), *kv_sum.parts()],
        smem=1,
        scratch=[pltpu.VMEM((2 * local, width), F32)],
    )
    n1g, n1s, n2g, n2s, out_bias_grad, down_bias_grad, up_bias_grad, q_bias_grad, v_bias_grad = outs
    return (
        output[None],
        input_grad[None],
        n1g,
        n1s,
        jnp.transpose(attn_grad.reshape(3, local, width), (2, 0, 1)),
        q_bias_grad,
        v_bias_grad,
        out_weight_grad,
        out_bias_grad,
        n2g,
        n2s,
        up_weight_grad,
        up_bias_grad,
        down_grad,
        down_bias_grad,
    )


def solution(mesh):
    row_spec = P("dp", ("ctx", "tensor"), None)
    return jax.shard_map(
        per_device,
        mesh=mesh,
        in_specs=(
            row_spec,
            P("dp", None),
            P(),
            P(),
            P(None, None, "tensor"),
            P("tensor"),
            P("tensor"),
            P("tensor", None),
            P(),
            P(),
            P(),
            P(None, "tensor"),
            P("tensor"),
            P("tensor", None),
            P(),
            row_spec,
        ),
        out_specs=(
            row_spec,
            row_spec,
            P(),
            P(),
            P(None, None, "tensor"),
            P("tensor"),
            P("tensor"),
            P("tensor", None),
            P(),
            P(),
            P(),
            P(None, "tensor"),
            P("tensor"),
            P("tensor", None),
            P(),
        ),
        check_vma=False,
    )
```

```python
import functools

import jax
import jax.numpy as jnp
from jax import lax
from jax.experimental import pallas as pl
from jax.experimental.pallas import tpu as pltpu
from jax.sharding import PartitionSpec as P

HEAD_DIM = 64
EPS = 1e-05
MASKED = -1e30
BF16 = jnp.bfloat16
F32 = jnp.float32
SCALE = HEAD_DIM**-0.5
LOG2_SCALE = SCALE * 1.4426950408889634
LONG_START_MAX = 128
LONG_END_MIN = 64 + 768
LONG_END_MAX = 128 + 768
MIB = 1024 * 1024


def dot(a, b, ca, cb):
    return lax.dot_general(a, b, (((ca,), (cb,)), ((), ())), preferred_element_type=F32)


def norm_parts(values):
    center = values - jnp.mean(values, axis=-1, keepdims=True)
    scale = lax.rsqrt(jnp.mean(center * center, axis=-1, keepdims=True) + EPS)
    return center * scale, scale


def norm_back(grad, gain, xhat, scale):
    g = grad * gain
    return scale * (
        g - jnp.mean(g, axis=-1, keepdims=True) - xhat * jnp.mean(g * xhat, axis=-1, keepdims=True)
    )


def xor_pairs(count, mask):
    return [(i, i ^ mask) for i in range(count)]


def pick(x, index):
    return lax.dynamic_index_in_dim(x, index, 0, keepdims=False)


def after(x, *deps):
    return lax.optimization_barrier((x,) + deps)[0]


def rows_at(index, size):
    return pl.ds(pl.multiple_of(index * size, size), size)


def call(kernel, out_shape, args, vmem=16, scratch=(), smem=0):
    spaces = [pltpu.SMEM] * smem + [pltpu.VMEM] * (len(args) - smem)
    return pl.pallas_call(
        kernel,
        out_shape=out_shape,
        in_specs=[pl.BlockSpec(memory_space=s) for s in spaces],
        out_specs=[pl.BlockSpec(memory_space=pltpu.VMEM)] * len(out_shape),
        scratch_shapes=list(scratch),
        compiler_params=pltpu.CompilerParams(vmem_limit_bytes=vmem * MIB),
    )(*args)


GAIN1, SHIFT1, QUERY_BIAS, VALUE_BIAS = range(4)
OUT_BIAS, GAIN2, SHIFT2, UP_BIAS, DOWN_BIAS = range(5)


def vec(ref, row, size=None):
    return ref[row : row + 1, :size]


def shape(dims, dtype):
    return jax.ShapeDtypeStruct(dims, dtype)


def pack_kernel(*refs):
    *vectors, vec_ref = refs
    for i, v in enumerate(vectors):
        vec_ref[i : i + 1, : v.shape[0]] = v[...].reshape(1, v.shape[0])


def first_kernel(meta_ref, *refs):
    vectors, (w_ref, x_ref, cot_ref, ow_ref) = refs[:4], refs[4:8]
    vec_ref, w_out, x_out, message = refs[8:]
    pack_kernel(*vectors, vec_ref)
    w_out[...] = w_ref[...]
    x_out[...] = x_ref[...]
    own = cot_ref.shape[0]
    message[:own] = cot_ref[...]
    message[own:] = ow_ref[rows_at(meta_ref[1], message.shape[0] - own)]


def qkv_kernel(
    meta_ref, x0, x1, x2, x3, vec_ref, w_ref, rows_ref, normed_ref, q_ref, kv_ref
):
    local = q_ref.shape[1]
    own = x0.shape[0]
    rank = meta_ref[0]
    gain, shift = vec(vec_ref, GAIN1), vec(vec_ref, SHIFT1)
    for r, x in enumerate((x0, x1, x2, x3)):
        at = rows_at(rank ^ r, own)
        rows_ref[at] = x[...]
        xhat, _ = norm_parts(x[...].astype(F32))
        normed_ref[at] = (xhat * gain + shift).astype(BF16)
    normed = normed_ref[...]
    q_ref[...] = (dot(normed, w_ref[:local], 1, 1) + vec(vec_ref, QUERY_BIAS, local)).astype(BF16)
    kv_ref[:, :local] = dot(normed, w_ref[local : 2 * local], 1, 1).astype(BF16)
    kv_ref[:, local:] = (dot(normed, w_ref[2 * local :], 1, 1) + vec(vec_ref, VALUE_BIAS, local)).astype(BF16)


def blocks_of(ctx, half, size):
    out = []
    for i in range(half // size):
        first = ctx * half + i * size
        low = LONG_END_MIN // 128 * 128 if first >= LONG_END_MAX else 0
        out.append((i * size, first, low, first + size))
    return out


def allowed_of(meta_ref, first, low, end, size):
    query = first + lax.broadcasted_iota(jnp.int32, (1, size), 1)
    start = jnp.zeros_like(query)
    bound = jnp.int32(0)
    for j in range(3):
        bound = bound + meta_ref[2 + j]
        start = jnp.where(query >= bound, bound, start)
    key = low + lax.broadcasted_iota(jnp.int32, (end - low, size), 0)
    return (key >= start) & (key <= query)


def head_mask(head, width):
    lane = lax.broadcasted_iota(jnp.int32, (1, width), 1)
    inside = (lane >= head * HEAD_DIM) & (lane < (head + 1) * HEAD_DIM)
    return jnp.where(inside, 1.0, 0.0).astype(BF16)


def attend_body(ctx, size, meta_ref, q_ref, k_ref, vt_ref, mix_ref, lse_ref):
    half, local = q_ref.shape
    for at, first, low, end in blocks_of(ctx, half, size):
        allowed = allowed_of(meta_ref, first, low, end, size)
        cols = slice(at, at + size)
        for h in range(local // HEAD_DIM):
            feats = slice(h * HEAD_DIM, (h + 1) * HEAD_DIM)
            q = q_ref[cols] * head_mask(h, local)
            s = dot(k_ref[low:end], q, 1, 1)
            s = jnp.where(allowed, s * LOG2_SCALE, MASKED)
            top = jnp.max(s, axis=0, keepdims=True)
            p = jnp.exp2(s - top)
            total = jnp.sum(p, axis=0, keepdims=True)
            p = p * (1.0 / total)
            lse_ref[h : h + 1, cols] = top + jnp.log2(total)
            mix = dot(vt_ref[feats, low:end], p.astype(BF16), 1, 0)
            mix_ref[feats, cols] = mix.astype(BF16)


def attend_kernel(size, meta_ref, q_ref, kv_ref, mix_ref, lse_ref, k_all, vt_all):
    half, local = q_ref.shape
    ctx = meta_ref[1]

    @pl.when(ctx == 0)
    def _():
        k_all[:half] = kv_ref[:half, :local]
        kvt = kv_ref[:half].T
        vt_all[:, :half] = kvt[local:]
        attend_body(0, size, meta_ref, q_ref, k_all, vt_all, mix_ref, lse_ref)

    @pl.when(ctx != 0)
    def _():
        k_all[...] = kv_ref[:, :local]
        kvt = kv_ref[...].T
        vt_all[...] = kvt[local:]
        attend_body(1, size, meta_ref, q_ref, k_all, vt_all, mix_ref, lse_ref)


def back_body(ctx, size, meta_ref, q_ref, d_ref, lse_ref, k_ref, kt_ref, v_ref, dq_ref, dk, dv, p_all, s_all):
    half, local = q_ref.shape
    heads = local // HEAD_DIM
    for at, first, low, end in blocks_of(ctx, half, size):
        allowed = allowed_of(meta_ref, first, low, end, size)
        cols = slice(at, at + size)
        keys = slice(low, end)
        qs, ds = [], []
        for h in range(heads):
            feats = slice(h * HEAD_DIM, (h + 1) * HEAD_DIM)
            mask = head_mask(h, local)
            q = q_ref[cols] * mask
            d = d_ref[cols] * mask
            qs.append(q)
            ds.append(d)
            s = dot(k_ref[keys], q, 1, 1)
            p = jnp.exp2(jnp.where(allowed, s * LOG2_SCALE - lse_ref[h : h + 1, cols], MASKED))
            dp = dot(v_ref[keys], d, 1, 1)
            center = jnp.sum(p * dp, axis=0, keepdims=True)
            score = (p * (dp - center)).astype(BF16)
            lanes = slice(h * size, (h + 1) * size)
            p_all[keys, lanes] = p.astype(BF16)
            s_all[keys, lanes] = score
            dq_ref[feats, cols] = (dot(kt_ref[feats, keys], score, 1, 0) * SCALE).astype(BF16)
        dk[keys] += dot(s_all[keys], jnp.concatenate(qs, 0), 1, 0)
        dv[keys] += dot(p_all[keys], jnp.concatenate(ds, 0), 1, 0)


def back_kernel(
    size, meta_ref, q_ref, kv_ref, lse_ref, b0, b1, b2, b3, w_ref,
    dq_ref, keep_ref, send_ref, rows_ref, k_all, kt_all, v_all, d_all, dk, dv, p_all, s_all,
):
    half, local = q_ref.shape
    own = b0.shape[0]
    rank, ctx = meta_ref[0], meta_ref[1]
    for r, b in enumerate((b0, b1, b2, b3)):
        rows_ref[rows_at(rank ^ r, own)] = b[...]
    d_all[...] = dot(rows_ref[...], w_ref[...], 1, 1).astype(BF16)
    rest = (dq_ref, dk, dv, p_all, s_all)

    @pl.when(ctx == 0)
    def _():
        k_all[:half] = kv_ref[:half, :local]
        v_all[:half] = kv_ref[:half, local:]
        kt_all[:, :half] = k_all[:half].T
        dk[:half] = jnp.zeros((half, local), F32)
        dv[:half] = jnp.zeros((half, local), F32)
        back_body(0, size, meta_ref, q_ref, d_all, lse_ref, k_all, kt_all, v_all, *rest)
        keep_ref[:, :local] = dk[:half] * SCALE
        keep_ref[:, local:] = dv[:half]
        send_ref[...] = jnp.zeros(send_ref.shape, BF16)

    @pl.when(ctx != 0)
    def _():
        k_all[...] = kv_ref[:, :local]
        v_all[...] = kv_ref[:, local:]
        kt_all[...] = k_all[...].T
        dk[...] = jnp.zeros(dk.shape, F32)
        dv[...] = jnp.zeros(dv.shape, F32)
        back_body(1, size, meta_ref, q_ref, d_all, lse_ref, k_all, kt_all, v_all, *rest)
        send_ref[:, :local] = (dk[:half] * SCALE).astype(BF16)
        send_ref[:, local:] = dv[:half].astype(BF16)
        keep_ref[:, :local] = dk[half:] * SCALE
        keep_ref[:, local:] = dv[half:]


def ff_kernel(
    meta_ref, m0, m1, m2, m3, x_ref, w_ref, wc_ref, vec_ref, up_ref, down_ref, c0, c1, c2, c3,
    normed_ref, active_ref, upg_ref, cot_ref, hidden_ref, s0, s1, s2, s3, ub_out, db_out, w_all, mix_all, part,
):
    own = c0.shape[0]
    half = x_ref.shape[0]
    local = w_ref.shape[0]
    rank, ctx = meta_ref[0], meta_ref[1]
    piece = local // 2
    w_all[:local] = w_ref[...]
    for r, c in enumerate((c1, c2, c3)):
        w_all[rows_at(2 * (r + 1) + ctx, piece)] = c[own:]
        w_all[rows_at(2 * (r + 1) + 1 - ctx, piece)] = wc_ref[rows_at(3 * (1 - ctx) + r, piece)]
    for r, m in enumerate((m0, m1, m2, m3)):
        mix_all[r * local : (r + 1) * local] = m[...]
    for r, c in enumerate((c0, c1, c2, c3)):
        cot_ref[rows_at(rank ^ r, own)] = c[:own]
    chunk = 256
    ob, gain, shift, ub = (vec(vec_ref, r) for r in (OUT_BIAS, GAIN2, SHIFT2, UP_BIAS))
    ub_total = jnp.zeros(ub_out.shape, F32)
    db_total = jnp.zeros(db_out.shape, F32)
    for i in range(half // chunk):
        at = slice(i * chunk, (i + 1) * chunk)
        hidden = dot(mix_all[:, at], w_all[...], 0, 0) + x_ref[at].astype(F32) + ob
        part[at] = hidden
        xhat, _ = norm_parts(hidden)
        normed_ref[at] = (xhat * gain + shift).astype(BF16)
    hidden_ref[...] = part[rows_at(rank, own)]
    for i in range(half // chunk):
        at = slice(i * chunk, (i + 1) * chunk)
        v = dot(normed_ref[at], up_ref[...], 1, 0) + ub
        d = dot(cot_ref[at], down_ref[...], 1, 1)
        square = v * v
        t = jnp.tanh(0.7978845608028654 * v * (1.0 + 0.044715 * square))
        active_ref[at] = (0.5 * v * (1.0 + t)).astype(BF16)
        slope = 0.5 * (1.0 + t) + (0.5 * 0.7978845608028654) * v * (1.0 - t * t) * (
            1.0 + 3.0 * 0.044715 * square
        )
        g = (d * slope).astype(BF16)
        upg_ref[at] = g
        ub_total += jnp.sum(g.astype(F32), axis=0, keepdims=True)
        db_total += jnp.sum(cot_ref[at].astype(F32), axis=0, keepdims=True)
        part[at] = dot(g, up_ref[...], 1, 1)
    ub_out[...] = ub_total
    db_out[...] = db_total
    s0[...] = part[rows_at(rank, own)]
    for r, s in enumerate((s1, s2, s3), 1):
        s[...] = part[rows_at(rank ^ r, own)].astype(BF16)


def quarters_out(meta_ref, total, quarters):
    ctx, bit = meta_ref[1], meta_ref[6]
    size = quarters[0].shape[0]
    own, near, far_near, far_own = quarters
    own[...] = total[rows_at(2 * ctx + bit, size)]
    near[...] = total[rows_at(2 * ctx + 1 - bit, size)]
    far_near[...] = total[rows_at(3 - 2 * ctx - bit, size)]
    far_own[...] = total[rows_at(2 - 2 * ctx + bit, size)]


def quarters_out3(meta_ref, total, quarters):
    own, near, far = quarters
    size = own.shape[0]
    quarters_out(meta_ref, total, (own, near, far.at[:size], far.at[size:]))


def weight_grad_kernel(meta_ref, a_ref, b_ref, *refs):
    total = refs[4]
    total[...] = dot(a_ref[...], b_ref[...], 0, 0).astype(BF16)
    quarters_out(meta_ref, total, refs[:4])


def out_part_kernel(meta_ref, active_ref, down_ref, s0, s2, first, part):
    rank = meta_ref[0]
    own = s0.shape[0]
    part[...] = dot(active_ref[...], down_ref[...], 1, 0)
    s0[...] = part[rows_at(rank, own)]
    s2[...] = part[rows_at(rank ^ 2, own)]
    first[:own] = part[rows_at(rank ^ 1, own)].astype(BF16)
    first[own:] = part[rows_at(rank ^ 3, own)].astype(BF16)


def out_second_kernel(s2, got, out_ref):
    own = s2.shape[0]
    out_ref[...] = (s2[...] + got[own:].astype(F32)).astype(BF16)


def output_kernel(s0, g1, g2, hidden_ref, vec_ref, out_ref):
    own = s0.shape[0]
    total = s0[...] + g1[:own].astype(F32) + g2[...].astype(F32)
    out_ref[...] = (hidden_ref[...] + total + vec(vec_ref, DOWN_BIAS)).astype(BF16)


def sum4(refs):
    total = refs[0][...]
    for ref in refs[1:]:
        total = total + ref[...].astype(F32)
    return total


def norm2_back_kernel(s0, g1, g2, g3, hidden_ref, cot_ref, vec_ref, grad_ref, low_ref, small_ref):
    grad = sum4((s0, g1, g2, g3))
    xhat, scale = norm_parts(hidden_ref[...])
    hidden_grad = cot_ref[...].astype(F32) + norm_back(grad, vec(vec_ref, GAIN2), xhat, scale)
    grad_ref[...] = hidden_grad
    low_ref[...] = hidden_grad.astype(BF16)
    small_ref[0:1] = jnp.sum(grad * xhat, axis=0, keepdims=True)
    small_ref[1:2] = jnp.sum(grad, axis=0, keepdims=True)


def q_back_kernel(
    meta_ref, dq_ref, normed_ref, mix_ref, rows_ref, t0, t1, t2, qb_ref, ob_ref, total
):
    local = dq_ref.shape[0]
    dq = dq_ref[...]
    total[:local] = dot(dq, normed_ref[...], 1, 0).astype(BF16)
    total[local:] = dot(mix_ref[...], rows_ref[...], 1, 0).astype(BF16)
    quarters_out3(meta_ref, total, (t0, t1, t2))
    qb_ref[...] = dot(jnp.ones((8, dq.shape[1]), BF16), dq, 1, 1)[0:1]
    ob_ref[...] = jnp.sum(rows_ref[...].astype(F32), axis=0, keepdims=True)


def kv_back_kernel(
    meta_ref, dq_ref, keep_kv, got_kv, normed_ref, w_ref, x_ref, norm2_ref,
    t0, t1, t2, s0, s2, first, norm_ref, vb_ref, total, part,
):
    rank, ctx = meta_ref[0], meta_ref[1]
    own, width = s0.shape
    half, local = keep_kv.shape[0], keep_kv.shape[1] // 2
    normed = normed_ref[...]
    dkv = (keep_kv[...] + got_kv[rows_at(1 - ctx, half)].astype(F32)).astype(BF16)
    total[...] = dot(dkv, normed, 0, 0).astype(BF16)
    quarters_out3(meta_ref, total, (t0, t1, t2))
    part[...] = dot(dq_ref[...], w_ref[:local], 0, 0) + dot(dkv, w_ref[local:], 1, 0)
    gain_total = jnp.zeros((1, width), F32)
    shift_total = jnp.zeros((1, width), F32)
    chunk = 128
    for c in range(half // chunk):
        at = slice(c * chunk, (c + 1) * chunk)
        xhat, _ = norm_parts(x_ref[at].astype(F32))
        gain_total += jnp.sum(part[at] * xhat, axis=0, keepdims=True)
        shift_total += jnp.sum(part[at], axis=0, keepdims=True)
    norms = jnp.concatenate(
        [gain_total, shift_total, norm2_ref[...], jnp.zeros((4, width), F32)], 0
    )
    norm_ref[...] = norms
    s0[...] = part[rows_at(rank, own)]
    s2[...] = part[rows_at(rank ^ 2, own)]
    first[:own] = part[rows_at(rank ^ 1, own)].astype(BF16)
    first[own : 2 * own] = part[rows_at(rank ^ 3, own)].astype(BF16)
    first[2 * own :] = high_low(norms)
    vb_ref[...] = jnp.sum(dkv.astype(F32), axis=0, keepdims=True)[:, local:]


def rows_second_kernel(s2, got, norm_ref, out_ref, norm_out):
    own = s2.shape[0]
    out_ref[:own] = (s2[...] + got[own : 2 * own].astype(F32)).astype(BF16)
    norms = norm_ref[...] + from_high_low(got[2 * own :])
    norm_out[...] = norms
    out_ref[own:] = high_low(norms)


def last_rows_kernel(
    s0, g1, g2, x_ref, vec1_ref, grad_ref, norm_ref, ob_ref, db_ref, ub_ref, qb_ref, vb_ref, in_out, small_ref
):
    own = s0.shape[0]
    grad = s0[...] + g1[:own].astype(F32) + g2[:own].astype(F32)
    norms = norm_ref[...] + from_high_low(g2[own:])
    xhat, scale = norm_parts(x_ref[...].astype(F32))
    grad = grad_ref[...] + norm_back(grad, vec(vec1_ref, GAIN1), xhat, scale)
    in_out[...] = grad.astype(BF16)
    local = qb_ref.shape[1]
    small_ref[0:4] = norms[:4]
    small_ref[4:5] = ob_ref[...]
    small_ref[5:6] = db_ref[...]
    small_ref[6:7] = ub_ref[...]
    small_ref[7:8] = jnp.zeros_like(ob_ref)
    small_ref[7:8, :local] = qb_ref[...]
    lanes = small_ref.shape[1] // 2
    small_ref[7:8, lanes : lanes + local] = vb_ref[...]


def peer_rows(ctx, pair_ref):
    return pair_ref[rows_at(1 - ctx, pair_ref.shape[0] // 2)]


def place(meta_ref, own_ref, other_ref, own_pair, other_peer, out_ref):
    ctx, bit = meta_ref[1], meta_ref[6]
    size = out_ref.shape[0] // 4
    out_ref[rows_at(2 * ctx + bit, size)] = own_ref[:size].astype(F32)
    out_ref[rows_at(2 * ctx + 1 - bit, size)] = other_ref[:size].astype(F32)
    out_ref[rows_at(2 - 2 * ctx + bit, size)] = peer_rows(ctx, own_pair)[:size].astype(F32)
    out_ref[rows_at(3 - 2 * ctx - bit, size)] = other_peer[:size].astype(F32)


def whole_kernel(meta_ref, *refs):
    place(meta_ref, *refs)


def attn_whole_kernel(meta_ref, *refs):
    qkv_out, out_out = refs[8:10]
    total = refs[19]
    local = out_out.shape[0]
    place(meta_ref, *refs[:4], total)
    qkv_out[:local] = total[:local]
    out_out[...] = total[local:]
    place(meta_ref, *refs[4:8], total)
    qkv_out[local:] = total[...]
    rows = total.shape[0] // 4
    tails = [r[rows:] for r in (refs[0], refs[1], refs[3])]
    tails.append(peer_rows(meta_ref[1], refs[2])[rows:])
    small = sum(from_high_low(t) for t in tails)
    outs = refs[10:19]
    for i, out in enumerate(outs[:7]):
        out[...] = small[i]
    lanes = small.shape[1] // 2
    outs[7][...] = small[7, :local]
    outs[8][...] = small[7, lanes : lanes + local]


def to_peers(blocks):
    return [
        lax.ppermute(b, "tensor", xor_pairs(lax.axis_size("tensor"), r))
        for r, b in enumerate(blocks, 1)
    ]


NEAR, FAR = xor_pairs(4, 1), xor_pairs(4, 2)
CTX = xor_pairs(2, 1)


def peer_add_kernel(meta_ref, a_ref, pair_ref, out_ref):
    size = a_ref.shape[0]
    got = pair_ref[rows_at(1 - meta_ref[1], size)].astype(F32)
    out_ref[...] = (a_ref[...].astype(F32) + got).astype(BF16)


def peer_add2_kernel(meta_ref, a_ref, b_ref, pair_ref, a_out, b_out):
    size = a_ref.shape[0]
    peer = 2 - 2 * meta_ref[1]
    a_out[...] = add(a_ref[...], pair_ref[rows_at(peer, size)]).astype(BF16)
    b_out[...] = add(b_ref[...], pair_ref[rows_at(peer + 1, size)]).astype(BF16)


def add(*parts):
    return sum((p.astype(F32) for p in parts[1:]), parts[0].astype(F32))


def high_low(x):
    high = x.astype(BF16).astype(F32)
    return jnp.concatenate([high, x - high], 0).astype(BF16)


def from_high_low(pair):
    pair = pair.astype(F32)
    return pair[:8] + pair[8:]


def sum_kernel(append, tailed, *refs):
    *ins, out_ref = refs
    if append:
        *ins, small_ref = ins
    rows = ins[0].shape[0] - (16 if tailed else 0)
    out_ref[:rows] = add(*(i[:rows] for i in ins)).astype(BF16)
    if append:
        out_ref[rows:] = high_low(small_ref[...])
    if tailed:
        out_ref[rows:] = high_low(sum(from_high_low(i[rows:]) for i in ins))


class Order:
    def __init__(self):
        self.last = None

    def first(self, x):
        return x if self.last is None else after(x, self.last)

    def call(self, kernel, out_shape, args, at=-1, **kw):
        args = list(args)
        args[at] = self.first(args[at])
        out = call(kernel, out_shape, args, **kw)
        self.last = out[0]
        return out

    def step(self, x):
        self.last = self.first(x)
        return self.last

    def pair(self, x):
        self.last = lax.all_gather(self.first(x), "ctx", axis=0, tiled=True)
        return self.last


class WeightSum:
    def __init__(self, order, meta, quarters):
        self.order, self.meta = order, meta
        if len(quarters) == 3:
            self.own, self.near, self.far = quarters
        else:
            self.own, self.near, self.far_near, self.far_own = quarters
        self.shape = [shape(self.own.shape, BF16)]
        self.short = lax.axis_size("dp") == 4

    def both(self):
        got = self.order.pair(self.far)
        send, self.own = self.order.call(
            peer_add2_kernel, self.shape * 2, [self.meta, self.near, self.own, got], smem=1
        )
        self.got = lax.ppermute(send, "dp", NEAR) if self.short else lax.psum(send, "dp")
        self.pair = None

    def one(self):
        got = self.order.pair(self.far_near)
        (send,) = self.order.call(
            peer_add_kernel, self.shape, [self.meta, self.near, got], smem=1
        )
        self.got = lax.ppermute(send, "dp", NEAR) if self.short else lax.psum(send, "dp")

        self.pair = lax.ppermute(self.far_own, "ctx", CTX)

    def three(self, small=None):
        other = self.got if self.short else jnp.zeros_like(self.got)
        args = [self.own, other] + ([] if self.pair is None else [self.pair])
        out = self.shape
        if small is not None:
            rows, cols = self.own.shape
            if not self.short:
                small = lax.psum(small, "dp")
                args = [lax.psum(add(*args).astype(BF16), "dp")]
                self.got = jnp.pad(self.got, ((0, 16), (0, 0)))
            args, out = args + [small], [shape((rows + 16, cols), BF16)]
        kernel = functools.partial(sum_kernel, small is not None, False)
        (self.own,) = self.order.call(kernel, out, args, at=0)
        if self.short:
            self.got = lax.ppermute(self.own, "dp", FAR)
        elif small is None:
            self.own = lax.psum(self.own, "dp")

    def four_add(self):
        if self.short:
            kernel = functools.partial(sum_kernel, False, self.own.shape != self.shape[0].shape)
            out = [shape(self.own.shape, BF16)]
            (self.own,) = self.order.call(kernel, out, [self.own, self.got], at=0)

    def four_send(self):
        if self.short:
            self.got = lax.ppermute(self.own, "dp", NEAR)

    def four(self):
        self.four_add()
        self.four_send()

    def five(self):
        self.own_pair = self.order.pair(self.own)

    def six(self):
        self.got_peer = lax.ppermute(self.got, "ctx", CTX)

    def parts(self):
        return [self.own, self.got, self.own_pair, self.got_peer]

    def whole(self):
        self.six()
        rows, cols = self.own.shape
        return self.order.call(
            whole_kernel, [shape((4 * rows, cols), F32)], [self.meta, *self.parts()], smem=1
        )[0]


def per_device(
    tokens,
    lengths,
    norm1_gain,
    norm1_shift,
    qkv_weight,
    query_bias,
    value_bias,
    out_weight,
    out_bias,
    norm2_gain,
    norm2_shift,
    up_weight,
    up_bias,
    down_weight,
    down_bias,
    cotangent,
):
    tokens, cotangent = tokens[0], cotangent[0]
    own, width = tokens.shape
    ranks = lax.axis_size("tensor")
    half = own * ranks
    full = half * lax.axis_size("ctx")
    local = qkv_weight.shape[2]
    hidden_units = up_weight.shape[1]
    rank = lax.axis_index("tensor")
    ctx = lax.axis_index("ctx")
    bit = lax.axis_index("dp") & 1
    meta = jnp.concatenate(
        [jnp.stack([rank, ctx]).astype(jnp.int32), lengths[0], bit.astype(jnp.int32)[None]]
    )
    weight_t = jnp.transpose(qkv_weight, (1, 2, 0)).reshape(3 * local, width)
    size = 128
    block = shape((own, width), F32)
    block_low = shape((own, width), BF16)
    row_out = shape((1, width), F32)

    def quarters(rows_all, cols):
        return [shape((rows_all // 4, cols), BF16)] * 4

    def quarters3(rows_all, cols):
        return quarters(rows_all, cols)[:2] + [shape((rows_all // 2, cols), BF16)]

    order = Order()
    xs = to_peers([tokens] * 3)
    vectors1, weight_t, own_x, message = call(
        first_kernel,
        [
            shape((8, width), F32),
            shape(weight_t.shape, BF16),
            block_low,
            shape((own + local // 2, width), BF16),
        ],
        [meta, norm1_gain, norm1_shift, query_bias, value_bias]
        + [weight_t, tokens, cotangent, out_weight],
        smem=1,
    )
    rows, normed1, q, kv = order.call(
        qkv_kernel,
        [shape((half, width), BF16)] * 2
        + [shape((half, local), BF16), shape((half, 2 * local), BF16)],
        [meta, own_x, *xs, vectors1, weight_t],
        smem=1,
    )
    cots = to_peers([after(message, *xs)] * 3)
    kv_all = order.pair(kv)
    mix, lse = order.call(
        functools.partial(attend_kernel, size),
        [shape((local, half), BF16), shape((8, half), F32)],
        [meta, q, kv_all],
        smem=1,
        scratch=[pltpu.VMEM((full, local), BF16), pltpu.VMEM((local, full), BF16)],
    )
    mixes = to_peers([mix] * 3)
    pieces = jnp.concatenate([after(cots[0], mix)[own:], cots[1][own:], cots[2][own:]], 0)
    pieces_ctx = order.pair(pieces)
    (vectors,) = order.call(
        pack_kernel,
        [shape((8, width), F32)],
        [out_bias, norm2_gain, norm2_shift, up_bias, down_bias],
    )
    (normed2, active, up_grad, cot_rows, hidden, *normed2_parts, up_bias_part, down_bias_part) = order.call(
        ff_kernel,
        [
            shape((half, width), BF16),
            shape((half, hidden_units), BF16),
            shape((half, hidden_units), BF16),
            shape((half, width), BF16),
            block,
            block,
            block_low,
            block_low,
            block_low,
            shape((1, hidden_units), F32),
            row_out,
        ],
        [meta, mix, *mixes, rows, out_weight, pieces_ctx, vectors]
        + [up_weight, down_weight, cotangent, *cots],
        smem=1,
        vmem=28,
        scratch=[
            pltpu.VMEM((ranks * local, width), BF16),
            pltpu.VMEM((ranks * local, half), BF16),
            pltpu.VMEM((half, width), F32),
        ],
    )
    normed2_got = to_peers(normed2_parts[1:])

    def weight_grad(a, b):
        rows_all, cols = a.shape[1], b.shape[1]
        out = order.call(
            weight_grad_kernel,
            quarters(rows_all, cols),
            [meta, a, b],
            smem=1,
            scratch=[pltpu.VMEM((rows_all, cols), BF16)],
        )
        return WeightSum(order, meta, out)

    down_sum = weight_grad(active, cot_rows)
    down_sum.one()
    up_sum = weight_grad(normed2, up_grad)
    hidden_grad, branch_grad, norm2_part = order.call(
        norm2_back_kernel,
        [block, block_low, shape((2, width), F32)],
        [normed2_parts[0], *normed2_got, hidden, cotangent, vectors],
        at=0,
    )
    branches = to_peers([branch_grad] * 3)
    up_sum.one()
    down_sum.three()
    o0, o2, o_first = order.call(
        out_part_kernel,
        [block, block, shape((2 * own, width), BF16)],
        [meta, active, down_weight],
        at=1,
        smem=1,
        scratch=[pltpu.VMEM((half, width), F32)],
    )
    dq, kv_keep, kv_send, branch_rows = order.call(
        functools.partial(back_kernel, size),
        [
            shape((local, half), BF16),
            shape((half, 2 * local), F32),
            shape((half, 2 * local), BF16),
            shape((half, width), BF16),
        ],
        [meta, q, kv_all, lse, branch_grad, *branches, out_weight],
        at=1,
        smem=1,
        vmem=24,
        scratch=[
            pltpu.VMEM((full, local), BF16),
            pltpu.VMEM((local, full), BF16),
            pltpu.VMEM((full, local), BF16),
            pltpu.VMEM((half, local), BF16),
            pltpu.VMEM((full, local), F32),
            pltpu.VMEM((full, local), F32),
            pltpu.VMEM((full, local // HEAD_DIM * size), BF16),
            pltpu.VMEM((full, local // HEAD_DIM * size), BF16),
        ],
    )
    kv_got = order.pair(kv_send)
    up_sum.three()
    down_sum.four_add()
    x_pairs, y_pairs = xor_pairs(ranks, 1), xor_pairs(ranks, 2)
    *kv_quarters, n0, n2, n_first, norm_part, v_bias_part = order.call(
        kv_back_kernel,
        quarters3(2 * local, width)
        + [block, block, shape((2 * own + 16, width), BF16)]
        + [shape((8, width), F32), shape((1, local), F32)],
        [meta, dq, kv_keep, kv_got, normed1, weight_t, rows, norm2_part],
        at=1,
        smem=1,
        scratch=[pltpu.VMEM((2 * local, width), BF16), pltpu.VMEM((half, width), F32)],
    )
    n_first_got = lax.ppermute(n_first, "tensor", x_pairs)
    kv_sum = WeightSum(order, meta, kv_quarters)
    kv_sum.both()
    *qo_quarters, q_bias_part, out_bias_part = order.call(
        q_back_kernel,
        quarters3(2 * local, width) + [shape((1, local), F32), row_out],
        [meta, dq, normed1, mix, branch_rows],
        at=1,
        smem=1,
        scratch=[pltpu.VMEM((2 * local, width), BF16)],
    )
    qo_sum = WeightSum(order, meta, qo_quarters)
    qo_sum.both()
    n_second, norm_part = order.call(
        rows_second_kernel,
        [shape((own + 16, width), BF16), shape((8, width), F32)],
        [n2, n_first_got, norm_part],
        at=0,
    )
    n_second_got = lax.ppermute(n_second, "tensor", y_pairs)
    kv_sum.three()
    up_sum.four_add()
    input_grad, small = order.call(
        last_rows_kernel,
        [block_low, shape((8, width), F32)],
        [n0, n_first_got, n_second_got, own_x, vectors1, hidden_grad, norm_part]
        + [out_bias_part, down_bias_part, up_bias_part, q_bias_part, v_bias_part],
        at=0,
    )
    qo_sum.three(small)
    down_sum.own = after(down_sum.own, qo_sum.own)
    down_sum.four_send()
    up_sum.own = after(up_sum.own, qo_sum.own)
    up_sum.four_send()
    o_first_got = lax.ppermute(after(o_first, small), "tensor", x_pairs)
    down_sum.five()
    up_sum.five()
    (o_second,) = order.call(out_second_kernel, [block_low], [o2, o_first_got], at=0)
    o_second_got = lax.ppermute(o_second, "tensor", y_pairs)
    down_sum.got = order.step(down_sum.got)
    up_sum.got = order.step(up_sum.got)
    kv_sum.four()
    qo_sum.four()
    kv_sum.five()
    qo_sum.five()
    kv_sum.got = order.step(kv_sum.got)
    qo_sum.got = order.step(qo_sum.got)
    down_grad = down_sum.whole()
    up_weight_grad = up_sum.whole()
    (output,) = order.call(
        output_kernel, [block_low], [o0, o_first_got, o_second_got, hidden, vectors], at=0
    )
    kv_sum.six()
    qo_sum.six()
    attn_grad, out_weight_grad, *outs = order.call(
        attn_whole_kernel,
        [shape((3 * local, width), F32), shape((local, width), F32)]
        + [shape((width,), F32)] * 7
        + [shape((local,), F32)] * 2,
        [meta, *qo_sum.parts(), *kv_sum.parts()],
        smem=1,
        scratch=[pltpu.VMEM((2 * local, width), F32)],
    )
    n1g, n1s, n2g, n2s, out_bias_grad, down_bias_grad, up_bias_grad, q_bias_grad, v_bias_grad = outs
    return (
        output[None],
        input_grad[None],
        n1g,
        n1s,
        jnp.transpose(attn_grad.reshape(3, local, width), (2, 0, 1)),
        q_bias_grad,
        v_bias_grad,
        out_weight_grad,
        out_bias_grad,
        n2g,
        n2s,
        up_weight_grad,
        up_bias_grad,
        down_grad,
        down_bias_grad,
    )


def solution(mesh):
    row_spec = P("dp", ("ctx", "tensor"), None)
    return jax.shard_map(
        per_device,
        mesh=mesh,
        in_specs=(
            row_spec,
            P("dp", None),
            P(),
            P(),
            P(None, None, "tensor"),
            P("tensor"),
            P("tensor"),
            P("tensor", None),
            P(),
            P(),
            P(),
            P(None, "tensor"),
            P("tensor"),
            P("tensor", None),
            P(),
            row_spec,
        ),
        out_specs=(
            row_spec,
            row_spec,
            P(),
            P(),
            P(None, None, "tensor"),
            P("tensor"),
            P("tensor"),
            P("tensor", None),
            P(),
            P(),
            P(),
            P(None, "tensor"),
            P("tensor"),
            P("tensor", None),
            P(),
        ),
        check_vma=False,
    )
```

```python
import functools

import jax
import jax.numpy as jnp
from jax import lax
from jax.experimental import pallas as pl
from jax.experimental.pallas import tpu as pltpu
from jax.sharding import PartitionSpec as P

HEAD_DIM = 64
EPS = 1e-05
MASKED = -1e30
BF16 = jnp.bfloat16
F32 = jnp.float32
SCALE = HEAD_DIM**-0.5
LOG2_SCALE = SCALE * 1.4426950408889634
LONG_START_MAX = 128
LONG_END_MIN = 64 + 768
LONG_END_MAX = 128 + 768
MIB = 1024 * 1024


def dot(a, b, ca, cb):
    return lax.dot_general(a, b, (((ca,), (cb,)), ((), ())), preferred_element_type=F32)


def norm_parts(values):
    center = values - jnp.mean(values, axis=-1, keepdims=True)
    scale = lax.rsqrt(jnp.mean(center * center, axis=-1, keepdims=True) + EPS)
    return center * scale, scale


def norm_back(grad, gain, xhat, scale):
    g = grad * gain
    return scale * (
        g - jnp.mean(g, axis=-1, keepdims=True) - xhat * jnp.mean(g * xhat, axis=-1, keepdims=True)
    )


def xor_pairs(count, mask):
    return [(i, i ^ mask) for i in range(count)]


def pick(x, index):
    return lax.dynamic_index_in_dim(x, index, 0, keepdims=False)


def after(x, *deps):
    return lax.optimization_barrier((x,) + deps)[0]


def rows_at(index, size):
    return pl.ds(pl.multiple_of(index * size, size), size)


def call(kernel, out_shape, args, vmem=16, scratch=(), smem=0):
    spaces = [pltpu.SMEM] * smem + [pltpu.VMEM] * (len(args) - smem)
    return pl.pallas_call(
        kernel,
        out_shape=out_shape,
        in_specs=[pl.BlockSpec(memory_space=s) for s in spaces],
        out_specs=[pl.BlockSpec(memory_space=pltpu.VMEM)] * len(out_shape),
        scratch_shapes=list(scratch),
        compiler_params=pltpu.CompilerParams(vmem_limit_bytes=vmem * MIB),
    )(*args)


GAIN1, SHIFT1, QUERY_BIAS, VALUE_BIAS = range(4)
OUT_BIAS, GAIN2, SHIFT2, UP_BIAS, DOWN_BIAS = range(5)


def vec(ref, row, size=None):
    return ref[row : row + 1, :size]


def shape(dims, dtype):
    return jax.ShapeDtypeStruct(dims, dtype)


def pack_kernel(*refs):
    *vectors, vec_ref = refs
    for i, v in enumerate(vectors):
        vec_ref[i : i + 1, : v.shape[0]] = v[...].reshape(1, v.shape[0])


def first_kernel(meta_ref, *refs):
    vectors, (w_ref, x_ref, cot_ref, ow_ref) = refs[:4], refs[4:8]
    vec_ref, w_out, x_out, message = refs[8:]
    pack_kernel(*vectors, vec_ref)
    w_out[...] = w_ref[...]
    x_out[...] = x_ref[...]
    own = cot_ref.shape[0]
    message[:own] = cot_ref[...]
    message[own:] = ow_ref[rows_at(meta_ref[1], message.shape[0] - own)]


def qkv_kernel(
    meta_ref, x0, x1, x2, x3, vec_ref, w_ref, rows_ref, normed_ref, q_ref, kv_ref
):
    local = q_ref.shape[1]
    own = x0.shape[0]
    rank = meta_ref[0]
    gain, shift = vec(vec_ref, GAIN1), vec(vec_ref, SHIFT1)
    for r, x in enumerate((x0, x1, x2, x3)):
        at = rows_at(rank ^ r, own)
        rows_ref[at] = x[...]
        xhat, _ = norm_parts(x[...].astype(F32))
        normed_ref[at] = (xhat * gain + shift).astype(BF16)
    normed = normed_ref[...]
    q_ref[...] = (dot(normed, w_ref[:local], 1, 1) + vec(vec_ref, QUERY_BIAS, local)).astype(BF16)
    kv_ref[:, :local] = dot(normed, w_ref[local : 2 * local], 1, 1).astype(BF16)
    kv_ref[:, local:] = (dot(normed, w_ref[2 * local :], 1, 1) + vec(vec_ref, VALUE_BIAS, local)).astype(BF16)


def blocks_of(ctx, half, size):
    out = []
    for i in range(half // size):
        first = ctx * half + i * size
        low = LONG_END_MIN // 128 * 128 if first >= LONG_END_MAX else 0
        out.append((i * size, first, low, first + size))
    return out


def allowed_of(meta_ref, first, low, end, size):
    query = first + lax.broadcasted_iota(jnp.int32, (1, size), 1)
    start = jnp.zeros_like(query)
    bound = jnp.int32(0)
    for j in range(3):
        bound = bound + meta_ref[2 + j]
        start = jnp.where(query >= bound, bound, start)
    key = low + lax.broadcasted_iota(jnp.int32, (end - low, size), 0)
    return (key >= start) & (key <= query)


def head_mask(head, width):
    lane = lax.broadcasted_iota(jnp.int32, (1, width), 1)
    inside = (lane >= head * HEAD_DIM) & (lane < (head + 1) * HEAD_DIM)
    return jnp.where(inside, 1.0, 0.0).astype(BF16)


def attend_body(ctx, size, meta_ref, q_ref, k_ref, vt_ref, mix_ref, lse_ref):
    half, local = q_ref.shape
    for at, first, low, end in blocks_of(ctx, half, size):
        allowed = allowed_of(meta_ref, first, low, end, size)
        cols = slice(at, at + size)
        for h in range(local // HEAD_DIM):
            feats = slice(h * HEAD_DIM, (h + 1) * HEAD_DIM)
            q = q_ref[cols] * head_mask(h, local)
            s = dot(k_ref[low:end], q, 1, 1)
            s = jnp.where(allowed, s * LOG2_SCALE, MASKED)
            top = jnp.max(s, axis=0, keepdims=True)
            p = jnp.exp2(s - top)
            total = jnp.sum(p, axis=0, keepdims=True)
            p = p * (1.0 / total)
            lse_ref[h : h + 1, cols] = top + jnp.log2(total)
            mix = dot(vt_ref[feats, low:end], p.astype(BF16), 1, 0)
            mix_ref[feats, cols] = mix.astype(BF16)


def attend_kernel(size, meta_ref, q_ref, kv_ref, mix_ref, lse_ref, k_all, vt_all):
    half, local = q_ref.shape
    ctx = meta_ref[1]

    @pl.when(ctx == 0)
    def _():
        k_all[:half] = kv_ref[:half, :local]
        kvt = kv_ref[:half].T
        vt_all[:, :half] = kvt[local:]
        attend_body(0, size, meta_ref, q_ref, k_all, vt_all, mix_ref, lse_ref)

    @pl.when(ctx != 0)
    def _():
        k_all[...] = kv_ref[:, :local]
        kvt = kv_ref[...].T
        vt_all[...] = kvt[local:]
        attend_body(1, size, meta_ref, q_ref, k_all, vt_all, mix_ref, lse_ref)


def back_body(ctx, size, meta_ref, q_ref, d_ref, lse_ref, k_ref, kt_ref, v_ref, dq_ref, dk, dv, p_all, s_all):
    half, local = q_ref.shape
    heads = local // HEAD_DIM
    for at, first, low, end in blocks_of(ctx, half, size):
        allowed = allowed_of(meta_ref, first, low, end, size)
        cols = slice(at, at + size)
        keys = slice(low, end)
        qs, ds = [], []
        for h in range(heads):
            feats = slice(h * HEAD_DIM, (h + 1) * HEAD_DIM)
            mask = head_mask(h, local)
            q = q_ref[cols] * mask
            d = d_ref[cols] * mask
            qs.append(q)
            ds.append(d)
            s = dot(k_ref[keys], q, 1, 1)
            p = jnp.exp2(jnp.where(allowed, s * LOG2_SCALE - lse_ref[h : h + 1, cols], MASKED))
            dp = dot(v_ref[keys], d, 1, 1)
            center = jnp.sum(p * dp, axis=0, keepdims=True)
            score = (p * (dp - center)).astype(BF16)
            lanes = slice(h * size, (h + 1) * size)
            p_all[keys, lanes] = p.astype(BF16)
            s_all[keys, lanes] = score
            dq_ref[feats, cols] = (dot(kt_ref[feats, keys], score, 1, 0) * SCALE).astype(BF16)
        dk[keys] += dot(s_all[keys], jnp.concatenate(qs, 0), 1, 0)
        dv[keys] += dot(p_all[keys], jnp.concatenate(ds, 0), 1, 0)


def back_kernel(
    size, meta_ref, q_ref, kv_ref, lse_ref, b0, b1, b2, b3, w_ref,
    dq_ref, keep_ref, send_ref, rows_ref, k_all, kt_all, v_all, d_all, dk, dv, p_all, s_all,
):
    half, local = q_ref.shape
    own = b0.shape[0]
    rank, ctx = meta_ref[0], meta_ref[1]
    for r, b in enumerate((b0, b1, b2, b3)):
        rows_ref[rows_at(rank ^ r, own)] = b[...]
    d_all[...] = dot(rows_ref[...], w_ref[...], 1, 1).astype(BF16)
    rest = (dq_ref, dk, dv, p_all, s_all)

    @pl.when(ctx == 0)
    def _():
        k_all[:half] = kv_ref[:half, :local]
        v_all[:half] = kv_ref[:half, local:]
        kt_all[:, :half] = k_all[:half].T
        dk[:half] = jnp.zeros((half, local), F32)
        dv[:half] = jnp.zeros((half, local), F32)
        back_body(0, size, meta_ref, q_ref, d_all, lse_ref, k_all, kt_all, v_all, *rest)
        keep_ref[:, :local] = dk[:half] * SCALE
        keep_ref[:, local:] = dv[:half]
        send_ref[...] = jnp.zeros(send_ref.shape, BF16)

    @pl.when(ctx != 0)
    def _():
        k_all[...] = kv_ref[:, :local]
        v_all[...] = kv_ref[:, local:]
        kt_all[...] = k_all[...].T
        dk[...] = jnp.zeros(dk.shape, F32)
        dv[...] = jnp.zeros(dv.shape, F32)
        back_body(1, size, meta_ref, q_ref, d_all, lse_ref, k_all, kt_all, v_all, *rest)
        send_ref[:, :local] = (dk[:half] * SCALE).astype(BF16)
        send_ref[:, local:] = dv[:half].astype(BF16)
        keep_ref[:, :local] = dk[half:] * SCALE
        keep_ref[:, local:] = dv[half:]


def ff_kernel(
    meta_ref, m0, m1, m2, m3, x_ref, w_ref, wc_ref, vec_ref, up_ref, down_ref, c0, c1, c2, c3,
    normed_ref, active_ref, upg_ref, cot_ref, hidden_ref, s0, s1, s2, s3, ub_out, db_out, w_all, mix_all, part,
):
    own = c0.shape[0]
    half = x_ref.shape[0]
    local = w_ref.shape[0]
    rank, ctx = meta_ref[0], meta_ref[1]
    piece = local // 2
    w_all[:local] = w_ref[...]
    for r, c in enumerate((c1, c2, c3)):
        w_all[rows_at(2 * (r + 1) + ctx, piece)] = c[own:]
        w_all[rows_at(2 * (r + 1) + 1 - ctx, piece)] = wc_ref[rows_at(3 * (1 - ctx) + r, piece)]
    for r, m in enumerate((m0, m1, m2, m3)):
        mix_all[r * local : (r + 1) * local] = m[...]
    for r, c in enumerate((c0, c1, c2, c3)):
        cot_ref[rows_at(rank ^ r, own)] = c[:own]
    chunk = 256
    ob, gain, shift, ub = (vec(vec_ref, r) for r in (OUT_BIAS, GAIN2, SHIFT2, UP_BIAS))
    ub_total = jnp.zeros(ub_out.shape, F32)
    db_total = jnp.zeros(db_out.shape, F32)
    for i in range(half // chunk):
        at = slice(i * chunk, (i + 1) * chunk)
        hidden = dot(mix_all[:, at], w_all[...], 0, 0) + x_ref[at].astype(F32) + ob
        part[at] = hidden
        xhat, _ = norm_parts(hidden)
        normed_ref[at] = (xhat * gain + shift).astype(BF16)
    hidden_ref[...] = part[rows_at(rank, own)]
    for i in range(half // chunk):
        at = slice(i * chunk, (i + 1) * chunk)
        v = dot(normed_ref[at], up_ref[...], 1, 0) + ub
        d = dot(cot_ref[at], down_ref[...], 1, 1)
        square = v * v
        t = jnp.tanh(0.7978845608028654 * v * (1.0 + 0.044715 * square))
        active_ref[at] = (0.5 * v * (1.0 + t)).astype(BF16)
        slope = 0.5 * (1.0 + t) + (0.5 * 0.7978845608028654) * v * (1.0 - t * t) * (
            1.0 + 3.0 * 0.044715 * square
        )
        g = (d * slope).astype(BF16)
        upg_ref[at] = g
        ub_total += jnp.sum(g.astype(F32), axis=0, keepdims=True)
        db_total += jnp.sum(cot_ref[at].astype(F32), axis=0, keepdims=True)
        part[at] = dot(g, up_ref[...], 1, 1)
    ub_out[...] = ub_total
    db_out[...] = db_total
    s0[...] = part[rows_at(rank, own)]
    for r, s in enumerate((s1, s2, s3), 1):
        s[...] = part[rows_at(rank ^ r, own)].astype(BF16)


def quarters_out(meta_ref, total, quarters):
    ctx, bit = meta_ref[1], meta_ref[6]
    size = quarters[0].shape[0]
    own, near, far_near, far_own = quarters
    own[...] = total[rows_at(2 * ctx + bit, size)]
    near[...] = total[rows_at(2 * ctx + 1 - bit, size)]
    far_near[...] = total[rows_at(3 - 2 * ctx - bit, size)]
    far_own[...] = total[rows_at(2 - 2 * ctx + bit, size)]


def quarters_out3(meta_ref, total, quarters):
    own, near, far = quarters
    size = own.shape[0]
    quarters_out(meta_ref, total, (own, near, far.at[:size], far.at[size:]))


def weight_grad_kernel(meta_ref, a_ref, b_ref, *refs):
    total = refs[4]
    total[...] = dot(a_ref[...], b_ref[...], 0, 0).astype(BF16)
    quarters_out(meta_ref, total, refs[:4])


def out_part_kernel(meta_ref, active_ref, down_ref, s0, s2, first, part):
    rank = meta_ref[0]
    own = s0.shape[0]
    part[...] = dot(active_ref[...], down_ref[...], 1, 0)
    s0[...] = part[rows_at(rank, own)]
    s2[...] = part[rows_at(rank ^ 2, own)]
    first[:own] = part[rows_at(rank ^ 1, own)].astype(BF16)
    first[own:] = part[rows_at(rank ^ 3, own)].astype(BF16)


def out_second_kernel(s2, got, out_ref):
    own = s2.shape[0]
    out_ref[...] = (s2[...] + got[own:].astype(F32)).astype(BF16)


def output_kernel(s0, g1, g2, hidden_ref, vec_ref, out_ref):
    own = s0.shape[0]
    total = s0[...] + g1[:own].astype(F32) + g2[...].astype(F32)
    out_ref[...] = (hidden_ref[...] + total + vec(vec_ref, DOWN_BIAS)).astype(BF16)


def sum4(refs):
    total = refs[0][...]
    for ref in refs[1:]:
        total = total + ref[...].astype(F32)
    return total


def norm2_back_kernel(s0, g1, g2, g3, hidden_ref, cot_ref, vec_ref, grad_ref, low_ref, small_ref):
    grad = sum4((s0, g1, g2, g3))
    xhat, scale = norm_parts(hidden_ref[...])
    hidden_grad = cot_ref[...].astype(F32) + norm_back(grad, vec(vec_ref, GAIN2), xhat, scale)
    grad_ref[...] = hidden_grad
    low_ref[...] = hidden_grad.astype(BF16)
    small_ref[0:1] = jnp.sum(grad * xhat, axis=0, keepdims=True)
    small_ref[1:2] = jnp.sum(grad, axis=0, keepdims=True)


def q_back_kernel(
    meta_ref, dq_ref, normed_ref, mix_ref, rows_ref, t0, t1, t2, qb_ref, ob_ref, total
):
    local = dq_ref.shape[0]
    dq = dq_ref[...]
    total[:local] = dot(dq, normed_ref[...], 1, 0).astype(BF16)
    total[local:] = dot(mix_ref[...], rows_ref[...], 1, 0).astype(BF16)
    quarters_out3(meta_ref, total, (t0, t1, t2))
    qb_ref[...] = dot(jnp.ones((8, dq.shape[1]), BF16), dq, 1, 1)[0:1]
    ob_ref[...] = jnp.sum(rows_ref[...].astype(F32), axis=0, keepdims=True)


def kv_back_kernel(
    meta_ref, dq_ref, keep_kv, got_kv, normed_ref, w_ref, x_ref, norm2_ref,
    t0, t1, t2, s0, s2, first, norm_ref, vb_ref, total, part,
):
    rank, ctx = meta_ref[0], meta_ref[1]
    own, width = s0.shape
    half, local = keep_kv.shape[0], keep_kv.shape[1] // 2
    normed = normed_ref[...]
    dkv = (keep_kv[...] + got_kv[rows_at(1 - ctx, half)].astype(F32)).astype(BF16)
    total[...] = dot(dkv, normed, 0, 0).astype(BF16)
    quarters_out3(meta_ref, total, (t0, t1, t2))
    part[...] = dot(dq_ref[...], w_ref[:local], 0, 0) + dot(dkv, w_ref[local:], 1, 0)
    gain_total = jnp.zeros((1, width), F32)
    shift_total = jnp.zeros((1, width), F32)
    chunk = 128
    for c in range(half // chunk):
        at = slice(c * chunk, (c + 1) * chunk)
        xhat, _ = norm_parts(x_ref[at].astype(F32))
        gain_total += jnp.sum(part[at] * xhat, axis=0, keepdims=True)
        shift_total += jnp.sum(part[at], axis=0, keepdims=True)
    norms = jnp.concatenate(
        [gain_total, shift_total, norm2_ref[...], jnp.zeros((4, width), F32)], 0
    )
    norm_ref[...] = norms
    s0[...] = part[rows_at(rank, own)]
    s2[...] = part[rows_at(rank ^ 2, own)]
    first[:own] = part[rows_at(rank ^ 1, own)].astype(BF16)
    first[own : 2 * own] = part[rows_at(rank ^ 3, own)].astype(BF16)
    first[2 * own :] = high_low(norms)
    vb_ref[...] = jnp.sum(dkv.astype(F32), axis=0, keepdims=True)[:, local:]


def rows_second_kernel(s2, got, norm_ref, out_ref, norm_out):
    own = s2.shape[0]
    out_ref[:own] = (s2[...] + got[own : 2 * own].astype(F32)).astype(BF16)
    norms = norm_ref[...] + from_high_low(got[2 * own :])
    norm_out[...] = norms
    out_ref[own:] = high_low(norms)


def last_rows_kernel(
    s0, g1, g2, x_ref, vec1_ref, grad_ref, norm_ref, ob_ref, db_ref, ub_ref, qb_ref, vb_ref, in_out, small_ref
):
    own = s0.shape[0]
    grad = s0[...] + g1[:own].astype(F32) + g2[:own].astype(F32)
    norms = norm_ref[...] + from_high_low(g2[own:])
    xhat, scale = norm_parts(x_ref[...].astype(F32))
    grad = grad_ref[...] + norm_back(grad, vec(vec1_ref, GAIN1), xhat, scale)
    in_out[...] = grad.astype(BF16)
    local = qb_ref.shape[1]
    small_ref[0:4] = norms[:4]
    small_ref[4:5] = ob_ref[...]
    small_ref[5:6] = db_ref[...]
    small_ref[6:7] = ub_ref[...]
    small_ref[7:8] = jnp.zeros_like(ob_ref)
    small_ref[7:8, :local] = qb_ref[...]
    lanes = small_ref.shape[1] // 2
    small_ref[7:8, lanes : lanes + local] = vb_ref[...]


def peer_rows(ctx, pair_ref):
    return pair_ref[rows_at(1 - ctx, pair_ref.shape[0] // 2)]


def place(meta_ref, own_ref, other_ref, own_pair, other_peer, out_ref):
    ctx, bit = meta_ref[1], meta_ref[6]
    size = out_ref.shape[0] // 4
    out_ref[rows_at(2 * ctx + bit, size)] = own_ref[:size].astype(F32)
    out_ref[rows_at(2 * ctx + 1 - bit, size)] = other_ref[:size].astype(F32)
    out_ref[rows_at(2 - 2 * ctx + bit, size)] = peer_rows(ctx, own_pair)[:size].astype(F32)
    other = other_peer if other_peer.shape[0] < 2 * size else peer_rows(ctx, other_peer)
    out_ref[rows_at(3 - 2 * ctx - bit, size)] = other[:size].astype(F32)


def whole_kernel(meta_ref, *refs):
    place(meta_ref, *refs)


def attn_whole_kernel(meta_ref, *refs):
    qkv_out, out_out = refs[8:10]
    total = refs[19]
    local = out_out.shape[0]
    place(meta_ref, *refs[:4], total)
    qkv_out[:local] = total[:local]
    out_out[...] = total[local:]
    place(meta_ref, *refs[4:8], total)
    qkv_out[local:] = total[...]
    rows = total.shape[0] // 4
    tails = [r[rows:] for r in (refs[0], refs[1], refs[3])]
    tails.append(peer_rows(meta_ref[1], refs[2])[rows:])
    small = sum(from_high_low(t) for t in tails)
    outs = refs[10:19]
    for i, out in enumerate(outs[:7]):
        out[...] = small[i]
    lanes = small.shape[1] // 2
    outs[7][...] = small[7, :local]
    outs[8][...] = small[7, lanes : lanes + local]


def to_peers(blocks):
    return [
        lax.ppermute(b, "tensor", xor_pairs(lax.axis_size("tensor"), r))
        for r, b in enumerate(blocks, 1)
    ]


NEAR, FAR = xor_pairs(4, 1), xor_pairs(4, 2)
CTX = xor_pairs(2, 1)


def peer_add_kernel(meta_ref, a_ref, pair_ref, out_ref):
    size = a_ref.shape[0]
    got = pair_ref[rows_at(1 - meta_ref[1], size)].astype(F32)
    out_ref[...] = (a_ref[...].astype(F32) + got).astype(BF16)


def peer_add2_kernel(meta_ref, a_ref, b_ref, pair_ref, a_out, b_out):
    size = a_ref.shape[0]
    peer = 2 - 2 * meta_ref[1]
    a_out[...] = add(a_ref[...], pair_ref[rows_at(peer, size)]).astype(BF16)
    b_out[...] = add(b_ref[...], pair_ref[rows_at(peer + 1, size)]).astype(BF16)


def add(*parts):
    return sum((p.astype(F32) for p in parts[1:]), parts[0].astype(F32))


def high_low(x):
    high = x.astype(BF16).astype(F32)
    return jnp.concatenate([high, x - high], 0).astype(BF16)


def from_high_low(pair):
    pair = pair.astype(F32)
    return pair[:8] + pair[8:]


def sum_kernel(append, tailed, *refs):
    *ins, out_ref = refs
    if append:
        *ins, small_ref = ins
    rows = ins[0].shape[0] - (16 if tailed else 0)
    out_ref[:rows] = add(*(i[:rows] for i in ins)).astype(BF16)
    if append:
        out_ref[rows:] = high_low(small_ref[...])
    if tailed:
        out_ref[rows:] = high_low(sum(from_high_low(i[rows:]) for i in ins))


class Order:
    def __init__(self):
        self.last = None

    def first(self, x):
        return x if self.last is None else after(x, self.last)

    def call(self, kernel, out_shape, args, at=-1, **kw):
        args = list(args)
        args[at] = self.first(args[at])
        out = call(kernel, out_shape, args, **kw)
        self.last = out[0]
        return out

    def step(self, x):
        self.last = self.first(x)
        return self.last

    def pair(self, x):
        self.last = lax.all_gather(self.first(x), "ctx", axis=0, tiled=True)
        return self.last


class WeightSum:
    def __init__(self, order, meta, quarters):
        self.order, self.meta = order, meta
        if len(quarters) == 3:
            self.own, self.near, self.far = quarters
        else:
            self.own, self.near, self.far_near, self.far_own = quarters
        self.shape = [shape(self.own.shape, BF16)]
        self.short = lax.axis_size("dp") == 4

    def both(self):
        got = self.order.pair(self.far)
        send, self.own = self.order.call(
            peer_add2_kernel, self.shape * 2, [self.meta, self.near, self.own, got], smem=1
        )
        self.got = lax.ppermute(send, "dp", NEAR) if self.short else lax.psum(send, "dp")
        self.pair = None

    def one(self):
        got = self.order.pair(self.far_near)
        (send,) = self.order.call(
            peer_add_kernel, self.shape, [self.meta, self.near, got], smem=1
        )
        self.got = lax.ppermute(send, "dp", NEAR) if self.short else lax.psum(send, "dp")

        self.pair = lax.ppermute(self.far_own, "ctx", CTX)

    def three(self, small=None):
        other = self.got if self.short else jnp.zeros_like(self.got)
        args = [self.own, other] + ([] if self.pair is None else [self.pair])
        out = self.shape
        if small is not None:
            rows, cols = self.own.shape
            if not self.short:
                small = lax.psum(small, "dp")
                args = [lax.psum(add(*args).astype(BF16), "dp")]
                self.got = jnp.pad(self.got, ((0, 16), (0, 0)))
            args, out = args + [small], [shape((rows + 16, cols), BF16)]
        kernel = functools.partial(sum_kernel, small is not None, False)
        (self.own,) = self.order.call(kernel, out, args, at=0)
        if self.short:
            self.got = lax.ppermute(self.own, "dp", FAR)
        elif small is None:
            self.own = lax.psum(self.own, "dp")

    def four_add(self):
        if self.short:
            kernel = functools.partial(sum_kernel, False, self.own.shape != self.shape[0].shape)
            out = [shape(self.own.shape, BF16)]
            (self.own,) = self.order.call(kernel, out, [self.own, self.got], at=0)

    def four_send(self):
        if self.short:
            self.got = lax.ppermute(self.own, "dp", NEAR)

    def four(self):
        self.four_add()
        self.four_send()

    def five(self):
        self.own_pair = self.order.pair(self.own)

    def six_now(self):
        self.got_peer = self.order.pair(self.got)

    def six(self):
        self.got_peer = lax.ppermute(self.got, "ctx", CTX)

    def parts(self):
        return [self.own, self.got, self.own_pair, self.got_peer]

    def whole(self):
        rows, cols = self.own.shape
        return self.order.call(
            whole_kernel, [shape((4 * rows, cols), F32)], [self.meta, *self.parts()], smem=1
        )[0]


def per_device(
    tokens,
    lengths,
    norm1_gain,
    norm1_shift,
    qkv_weight,
    query_bias,
    value_bias,
    out_weight,
    out_bias,
    norm2_gain,
    norm2_shift,
    up_weight,
    up_bias,
    down_weight,
    down_bias,
    cotangent,
):
    tokens, cotangent = tokens[0], cotangent[0]
    own, width = tokens.shape
    ranks = lax.axis_size("tensor")
    half = own * ranks
    full = half * lax.axis_size("ctx")
    local = qkv_weight.shape[2]
    hidden_units = up_weight.shape[1]
    rank = lax.axis_index("tensor")
    ctx = lax.axis_index("ctx")
    bit = lax.axis_index("dp") & 1
    meta = jnp.concatenate(
        [jnp.stack([rank, ctx]).astype(jnp.int32), lengths[0], bit.astype(jnp.int32)[None]]
    )
    weight_t = jnp.transpose(qkv_weight, (1, 2, 0)).reshape(3 * local, width)
    size = 128
    block = shape((own, width), F32)
    block_low = shape((own, width), BF16)
    row_out = shape((1, width), F32)

    def quarters(rows_all, cols):
        return [shape((rows_all // 4, cols), BF16)] * 4

    def quarters3(rows_all, cols):
        return quarters(rows_all, cols)[:2] + [shape((rows_all // 2, cols), BF16)]

    order = Order()
    xs = to_peers([tokens] * 3)
    vectors1, weight_t, own_x, message = call(
        first_kernel,
        [
            shape((8, width), F32),
            shape(weight_t.shape, BF16),
            block_low,
            shape((own + local // 2, width), BF16),
        ],
        [meta, norm1_gain, norm1_shift, query_bias, value_bias]
        + [weight_t, tokens, cotangent, out_weight],
        smem=1,
    )
    rows, normed1, q, kv = order.call(
        qkv_kernel,
        [shape((half, width), BF16)] * 2
        + [shape((half, local), BF16), shape((half, 2 * local), BF16)],
        [meta, own_x, *xs, vectors1, weight_t],
        smem=1,
    )
    cots = to_peers([after(message, *xs)] * 3)
    kv_all = order.pair(kv)
    mix, lse = order.call(
        functools.partial(attend_kernel, size),
        [shape((local, half), BF16), shape((8, half), F32)],
        [meta, q, kv_all],
        smem=1,
        scratch=[pltpu.VMEM((full, local), BF16), pltpu.VMEM((local, full), BF16)],
    )
    mixes = to_peers([mix] * 3)
    pieces = jnp.concatenate([after(cots[0], mix)[own:], cots[1][own:], cots[2][own:]], 0)
    pieces_ctx = order.pair(pieces)
    (vectors,) = order.call(
        pack_kernel,
        [shape((8, width), F32)],
        [out_bias, norm2_gain, norm2_shift, up_bias, down_bias],
    )
    (normed2, active, up_grad, cot_rows, hidden, *normed2_parts, up_bias_part, down_bias_part) = order.call(
        ff_kernel,
        [
            shape((half, width), BF16),
            shape((half, hidden_units), BF16),
            shape((half, hidden_units), BF16),
            shape((half, width), BF16),
            block,
            block,
            block_low,
            block_low,
            block_low,
            shape((1, hidden_units), F32),
            row_out,
        ],
        [meta, mix, *mixes, rows, out_weight, pieces_ctx, vectors]
        + [up_weight, down_weight, cotangent, *cots],
        smem=1,
        vmem=28,
        scratch=[
            pltpu.VMEM((ranks * local, width), BF16),
            pltpu.VMEM((ranks * local, half), BF16),
            pltpu.VMEM((half, width), F32),
        ],
    )
    normed2_got = to_peers(normed2_parts[1:])

    def weight_grad(a, b):
        rows_all, cols = a.shape[1], b.shape[1]
        out = order.call(
            weight_grad_kernel,
            quarters(rows_all, cols),
            [meta, a, b],
            smem=1,
            scratch=[pltpu.VMEM((rows_all, cols), BF16)],
        )
        return WeightSum(order, meta, out)

    down_sum = weight_grad(active, cot_rows)
    down_sum.one()
    up_sum = weight_grad(normed2, up_grad)
    hidden_grad, branch_grad, norm2_part = order.call(
        norm2_back_kernel,
        [block, block_low, shape((2, width), F32)],
        [normed2_parts[0], *normed2_got, hidden, cotangent, vectors],
        at=0,
    )
    branches = to_peers([branch_grad] * 3)
    up_sum.one()
    down_sum.three()
    o0, o2, o_first = order.call(
        out_part_kernel,
        [block, block, shape((2 * own, width), BF16)],
        [meta, active, down_weight],
        at=1,
        smem=1,
        scratch=[pltpu.VMEM((half, width), F32)],
    )
    dq, kv_keep, kv_send, branch_rows = order.call(
        functools.partial(back_kernel, size),
        [
            shape((local, half), BF16),
            shape((half, 2 * local), F32),
            shape((half, 2 * local), BF16),
            shape((half, width), BF16),
        ],
        [meta, q, kv_all, lse, branch_grad, *branches, out_weight],
        at=1,
        smem=1,
        vmem=24,
        scratch=[
            pltpu.VMEM((full, local), BF16),
            pltpu.VMEM((local, full), BF16),
            pltpu.VMEM((full, local), BF16),
            pltpu.VMEM((half, local), BF16),
            pltpu.VMEM((full, local), F32),
            pltpu.VMEM((full, local), F32),
            pltpu.VMEM((full, local // HEAD_DIM * size), BF16),
            pltpu.VMEM((full, local // HEAD_DIM * size), BF16),
        ],
    )
    kv_got = order.pair(kv_send)
    up_sum.three()
    down_sum.four_add()
    x_pairs, y_pairs = xor_pairs(ranks, 1), xor_pairs(ranks, 2)
    *kv_quarters, n0, n2, n_first, norm_part, v_bias_part = order.call(
        kv_back_kernel,
        quarters3(2 * local, width)
        + [block, block, shape((2 * own + 16, width), BF16)]
        + [shape((8, width), F32), shape((1, local), F32)],
        [meta, dq, kv_keep, kv_got, normed1, weight_t, rows, norm2_part],
        at=1,
        smem=1,
        scratch=[pltpu.VMEM((2 * local, width), BF16), pltpu.VMEM((half, width), F32)],
    )
    n_first_got = lax.ppermute(n_first, "tensor", x_pairs)
    kv_sum = WeightSum(order, meta, kv_quarters)
    kv_sum.both()
    *qo_quarters, q_bias_part, out_bias_part = order.call(
        q_back_kernel,
        quarters3(2 * local, width) + [shape((1, local), F32), row_out],
        [meta, dq, normed1, mix, branch_rows],
        at=1,
        smem=1,
        scratch=[pltpu.VMEM((2 * local, width), BF16)],
    )
    qo_sum = WeightSum(order, meta, qo_quarters)
    qo_sum.both()
    n_second, norm_part = order.call(
        rows_second_kernel,
        [shape((own + 16, width), BF16), shape((8, width), F32)],
        [n2, n_first_got, norm_part],
        at=0,
    )
    n_second_got = lax.ppermute(n_second, "tensor", y_pairs)
    kv_sum.three()
    up_sum.four_add()
    input_grad, small = order.call(
        last_rows_kernel,
        [block_low, shape((8, width), F32)],
        [n0, n_first_got, n_second_got, own_x, vectors1, hidden_grad, norm_part]
        + [out_bias_part, down_bias_part, up_bias_part, q_bias_part, v_bias_part],
        at=0,
    )
    qo_sum.three(small)
    down_sum.own = after(down_sum.own, qo_sum.own)
    down_sum.four_send()
    up_sum.own = after(up_sum.own, qo_sum.own)
    up_sum.four_send()
    o_first_got = lax.ppermute(after(o_first, small), "tensor", x_pairs)
    down_sum.five()
    up_sum.five()
    (o_second,) = order.call(out_second_kernel, [block_low], [o2, o_first_got], at=0)
    o_second_got = lax.ppermute(o_second, "tensor", y_pairs)
    down_sum.got = order.step(down_sum.got)
    down_sum.six_now()
    down_grad = down_sum.whole()
    up_sum.got = order.step(up_sum.got)
    kv_sum.four()
    qo_sum.four()
    kv_sum.five()
    qo_sum.five()
    kv_sum.got = order.step(kv_sum.got)
    qo_sum.got = order.step(qo_sum.got)
    up_sum.six()
    up_weight_grad = up_sum.whole()
    (output,) = order.call(
        output_kernel, [block_low], [o0, o_first_got, o_second_got, hidden, vectors], at=0
    )
    kv_sum.six()
    qo_sum.six()
    attn_grad, out_weight_grad, *outs = order.call(
        attn_whole_kernel,
        [shape((3 * local, width), F32), shape((local, width), F32)]
        + [shape((width,), F32)] * 7
        + [shape((local,), F32)] * 2,
        [meta, *qo_sum.parts(), *kv_sum.parts()],
        smem=1,
        scratch=[pltpu.VMEM((2 * local, width), F32)],
    )
    n1g, n1s, n2g, n2s, out_bias_grad, down_bias_grad, up_bias_grad, q_bias_grad, v_bias_grad = outs
    return (
        output[None],
        input_grad[None],
        n1g,
        n1s,
        jnp.transpose(attn_grad.reshape(3, local, width), (2, 0, 1)),
        q_bias_grad,
        v_bias_grad,
        out_weight_grad,
        out_bias_grad,
        n2g,
        n2s,
        up_weight_grad,
        up_bias_grad,
        down_grad,
        down_bias_grad,
    )


def solution(mesh):
    row_spec = P("dp", ("ctx", "tensor"), None)
    return jax.shard_map(
        per_device,
        mesh=mesh,
        in_specs=(
            row_spec,
            P("dp", None),
            P(),
            P(),
            P(None, None, "tensor"),
            P("tensor"),
            P("tensor"),
            P("tensor", None),
            P(),
            P(),
            P(),
            P(None, "tensor"),
            P("tensor"),
            P("tensor", None),
            P(),
            row_spec,
        ),
        out_specs=(
            row_spec,
            row_spec,
            P(),
            P(),
            P(None, None, "tensor"),
            P("tensor"),
            P("tensor"),
            P("tensor", None),
            P(),
            P(),
            P(),
            P(None, "tensor"),
            P("tensor"),
            P("tensor", None),
            P(),
        ),
        check_vma=False,
    )
```

```python
import functools

import jax
import jax.numpy as jnp
from jax import lax
from jax.experimental import pallas as pl
from jax.experimental.pallas import tpu as pltpu
from jax.sharding import PartitionSpec as P

HEAD_DIM = 64
EPS = 1e-05
MASKED = -1e30
BF16 = jnp.bfloat16
F32 = jnp.float32
SCALE = HEAD_DIM**-0.5
LOG2_SCALE = SCALE * 1.4426950408889634
LONG_START_MAX = 128
LONG_END_MIN = 64 + 768
LONG_END_MAX = 128 + 768
MIB = 1024 * 1024


def dot(a, b, ca, cb):
    return lax.dot_general(a, b, (((ca,), (cb,)), ((), ())), preferred_element_type=F32)


def norm_parts(values):
    center = values - jnp.mean(values, axis=-1, keepdims=True)
    scale = lax.rsqrt(jnp.mean(center * center, axis=-1, keepdims=True) + EPS)
    return center * scale, scale


def norm_back(grad, gain, xhat, scale):
    g = grad * gain
    return scale * (
        g - jnp.mean(g, axis=-1, keepdims=True) - xhat * jnp.mean(g * xhat, axis=-1, keepdims=True)
    )


def xor_pairs(count, mask):
    return [(i, i ^ mask) for i in range(count)]


def pick(x, index):
    return lax.dynamic_index_in_dim(x, index, 0, keepdims=False)


def after(x, *deps):
    return lax.optimization_barrier((x,) + deps)[0]


def rows_at(index, size):
    return pl.ds(pl.multiple_of(index * size, size), size)


def call(kernel, out_shape, args, vmem=16, scratch=(), smem=0):
    spaces = [pltpu.SMEM] * smem + [pltpu.VMEM] * (len(args) - smem)
    return pl.pallas_call(
        kernel,
        out_shape=out_shape,
        in_specs=[pl.BlockSpec(memory_space=s) for s in spaces],
        out_specs=[pl.BlockSpec(memory_space=pltpu.VMEM)] * len(out_shape),
        scratch_shapes=list(scratch),
        compiler_params=pltpu.CompilerParams(vmem_limit_bytes=vmem * MIB),
    )(*args)


GAIN1, SHIFT1, QUERY_BIAS, VALUE_BIAS = range(4)
OUT_BIAS, GAIN2, SHIFT2, UP_BIAS, DOWN_BIAS = range(5)


def vec(ref, row, size=None):
    return ref[row : row + 1, :size]


def shape(dims, dtype):
    return jax.ShapeDtypeStruct(dims, dtype)


def pack_kernel(*refs):
    *vectors, vec_ref = refs
    for i, v in enumerate(vectors):
        vec_ref[i : i + 1, : v.shape[0]] = v[...].reshape(1, v.shape[0])


def first_kernel(meta_ref, *refs):
    vectors, (w_ref, x_ref, cot_ref, ow_ref) = refs[:4], refs[4:8]
    vec_ref, w_out, x_out, message = refs[8:]
    pack_kernel(*vectors, vec_ref)
    w_out[...] = w_ref[...]
    x_out[...] = x_ref[...]
    own = cot_ref.shape[0]
    message[:own] = cot_ref[...]
    message[own:] = ow_ref[rows_at(meta_ref[1], message.shape[0] - own)]


def qkv_kernel(
    meta_ref, x0, x1, x2, x3, vec_ref, w_ref, rows_ref, normed_ref, q_ref, kv_ref
):
    local = q_ref.shape[1]
    own = x0.shape[0]
    rank = meta_ref[0]
    gain, shift = vec(vec_ref, GAIN1), vec(vec_ref, SHIFT1)
    for r, x in enumerate((x0, x1, x2, x3)):
        at = rows_at(rank ^ r, own)
        rows_ref[at] = x[...]
        xhat, _ = norm_parts(x[...].astype(F32))
        normed_ref[at] = (xhat * gain + shift).astype(BF16)
    normed = normed_ref[...]
    q_ref[...] = (dot(normed, w_ref[:local], 1, 1) + vec(vec_ref, QUERY_BIAS, local)).astype(BF16)
    kv_ref[:, :local] = dot(normed, w_ref[local : 2 * local], 1, 1).astype(BF16)
    kv_ref[:, local:] = (dot(normed, w_ref[2 * local :], 1, 1) + vec(vec_ref, VALUE_BIAS, local)).astype(BF16)


def blocks_of(ctx, half, size):
    out = []
    for i in range(half // size):
        first = ctx * half + i * size
        low = LONG_END_MIN // 128 * 128 if first >= LONG_END_MAX else 0
        out.append((i * size, first, low, first + size))
    return out


def allowed_of(meta_ref, first, low, end, size):
    query = first + lax.broadcasted_iota(jnp.int32, (1, size), 1)
    start = jnp.zeros_like(query)
    bound = jnp.int32(0)
    for j in range(3):
        bound = bound + meta_ref[2 + j]
        start = jnp.where(query >= bound, bound, start)
    key = low + lax.broadcasted_iota(jnp.int32, (end - low, size), 0)
    return (key >= start) & (key <= query)


def head_mask(head, width):
    lane = lax.broadcasted_iota(jnp.int32, (1, width), 1)
    inside = (lane >= head * HEAD_DIM) & (lane < (head + 1) * HEAD_DIM)
    return jnp.where(inside, 1.0, 0.0).astype(BF16)


def attend_body(ctx, size, meta_ref, q_ref, k_ref, vt_ref, mix_ref, lse_ref):
    half, local = q_ref.shape
    for at, first, low, end in blocks_of(ctx, half, size):
        allowed = allowed_of(meta_ref, first, low, end, size)
        cols = slice(at, at + size)
        for h in range(local // HEAD_DIM):
            feats = slice(h * HEAD_DIM, (h + 1) * HEAD_DIM)
            q = q_ref[cols] * head_mask(h, local)
            s = dot(k_ref[low:end], q, 1, 1)
            s = jnp.where(allowed, s * LOG2_SCALE, MASKED)
            top = jnp.max(s, axis=0, keepdims=True)
            p = jnp.exp2(s - top)
            total = jnp.sum(p, axis=0, keepdims=True)
            p = p * (1.0 / total)
            lse_ref[h : h + 1, cols] = top + jnp.log2(total)
            mix = dot(vt_ref[feats, low:end], p.astype(BF16), 1, 0)
            mix_ref[feats, cols] = mix.astype(BF16)


def attend_kernel(size, meta_ref, q_ref, kv_ref, mix_ref, lse_ref, k_all, vt_all):
    half, local = q_ref.shape
    ctx = meta_ref[1]

    @pl.when(ctx == 0)
    def _():
        k_all[:half] = kv_ref[:half, :local]
        kvt = kv_ref[:half].T
        vt_all[:, :half] = kvt[local:]
        attend_body(0, size, meta_ref, q_ref, k_all, vt_all, mix_ref, lse_ref)

    @pl.when(ctx != 0)
    def _():
        k_all[...] = kv_ref[:, :local]
        kvt = kv_ref[...].T
        vt_all[...] = kvt[local:]
        attend_body(1, size, meta_ref, q_ref, k_all, vt_all, mix_ref, lse_ref)


def back_body(ctx, size, meta_ref, q_ref, d_ref, lse_ref, k_ref, kt_ref, v_ref, dq_ref, dk, dv, p_all, s_all):
    half, local = q_ref.shape
    heads = local // HEAD_DIM
    for at, first, low, end in blocks_of(ctx, half, size):
        allowed = allowed_of(meta_ref, first, low, end, size)
        cols = slice(at, at + size)
        keys = slice(low, end)
        qs, ds = [], []
        for h in range(heads):
            feats = slice(h * HEAD_DIM, (h + 1) * HEAD_DIM)
            mask = head_mask(h, local)
            q = q_ref[cols] * mask
            d = d_ref[cols] * mask
            qs.append(q)
            ds.append(d)
            s = dot(k_ref[keys], q, 1, 1)
            p = jnp.exp2(jnp.where(allowed, s * LOG2_SCALE - lse_ref[h : h + 1, cols], MASKED))
            dp = dot(v_ref[keys], d, 1, 1)
            center = jnp.sum(p * dp, axis=0, keepdims=True)
            score = (p * (dp - center)).astype(BF16)
            lanes = slice(h * size, (h + 1) * size)
            p_all[keys, lanes] = p.astype(BF16)
            s_all[keys, lanes] = score
            dq_ref[feats, cols] = (dot(kt_ref[feats, keys], score, 1, 0) * SCALE).astype(BF16)
        dk[keys] += dot(s_all[keys], jnp.concatenate(qs, 0), 1, 0)
        dv[keys] += dot(p_all[keys], jnp.concatenate(ds, 0), 1, 0)


def back_kernel(
    size, meta_ref, q_ref, kv_ref, lse_ref, b0, b1, b2, b3, w_ref,
    dq_ref, keep_ref, send_ref, rows_ref, k_all, kt_all, v_all, d_all, dk, dv, p_all, s_all,
):
    half, local = q_ref.shape
    own = b0.shape[0]
    rank, ctx = meta_ref[0], meta_ref[1]
    for r, b in enumerate((b0, b1, b2, b3)):
        rows_ref[rows_at(rank ^ r, own)] = b[...]
    d_all[...] = dot(rows_ref[...], w_ref[...], 1, 1).astype(BF16)
    rest = (dq_ref, dk, dv, p_all, s_all)

    @pl.when(ctx == 0)
    def _():
        k_all[:half] = kv_ref[:half, :local]
        v_all[:half] = kv_ref[:half, local:]
        kt_all[:, :half] = k_all[:half].T
        dk[:half] = jnp.zeros((half, local), F32)
        dv[:half] = jnp.zeros((half, local), F32)
        back_body(0, size, meta_ref, q_ref, d_all, lse_ref, k_all, kt_all, v_all, *rest)
        keep_ref[:, :local] = dk[:half] * SCALE
        keep_ref[:, local:] = dv[:half]
        send_ref[...] = jnp.zeros(send_ref.shape, BF16)

    @pl.when(ctx != 0)
    def _():
        k_all[...] = kv_ref[:, :local]
        v_all[...] = kv_ref[:, local:]
        kt_all[...] = k_all[...].T
        dk[...] = jnp.zeros(dk.shape, F32)
        dv[...] = jnp.zeros(dv.shape, F32)
        back_body(1, size, meta_ref, q_ref, d_all, lse_ref, k_all, kt_all, v_all, *rest)
        send_ref[:, :local] = (dk[:half] * SCALE).astype(BF16)
        send_ref[:, local:] = dv[:half].astype(BF16)
        keep_ref[:, :local] = dk[half:] * SCALE
        keep_ref[:, local:] = dv[half:]


def ff_kernel(
    meta_ref, m0, m1, m2, m3, x_ref, w_ref, wc_ref, vec_ref, up_ref, down_ref, c0, c1, c2, c3,
    normed_ref, active_ref, upg_ref, cot_ref, hidden_ref, s0, s1, s2, s3, ub_out, db_out, w_all, mix_all, part,
):
    own = c0.shape[0]
    half = x_ref.shape[0]
    local = w_ref.shape[0]
    rank, ctx = meta_ref[0], meta_ref[1]
    piece = local // 2
    w_all[:local] = w_ref[...]
    for r, c in enumerate((c1, c2, c3)):
        w_all[rows_at(2 * (r + 1) + ctx, piece)] = c[own:]
        w_all[rows_at(2 * (r + 1) + 1 - ctx, piece)] = wc_ref[rows_at(3 * (1 - ctx) + r, piece)]
    for r, m in enumerate((m0, m1, m2, m3)):
        mix_all[r * local : (r + 1) * local] = m[...]
    for r, c in enumerate((c0, c1, c2, c3)):
        cot_ref[rows_at(rank ^ r, own)] = c[:own]
    chunk = 256
    ob, gain, shift, ub = (vec(vec_ref, r) for r in (OUT_BIAS, GAIN2, SHIFT2, UP_BIAS))
    ub_total = jnp.zeros(ub_out.shape, F32)
    db_total = jnp.zeros(db_out.shape, F32)
    for i in range(half // chunk):
        at = slice(i * chunk, (i + 1) * chunk)
        hidden = dot(mix_all[:, at], w_all[...], 0, 0) + x_ref[at].astype(F32) + ob
        part[at] = hidden
        xhat, _ = norm_parts(hidden)
        normed_ref[at] = (xhat * gain + shift).astype(BF16)
    hidden_ref[...] = part[rows_at(rank, own)]
    for i in range(half // chunk):
        at = slice(i * chunk, (i + 1) * chunk)
        v = dot(normed_ref[at], up_ref[...], 1, 0) + ub
        d = dot(cot_ref[at], down_ref[...], 1, 1)
        square = v * v
        t = jnp.tanh(0.7978845608028654 * v * (1.0 + 0.044715 * square))
        active_ref[at] = (0.5 * v * (1.0 + t)).astype(BF16)
        slope = 0.5 * (1.0 + t) + (0.5 * 0.7978845608028654) * v * (1.0 - t * t) * (
            1.0 + 3.0 * 0.044715 * square
        )
        g = (d * slope).astype(BF16)
        upg_ref[at] = g
        ub_total += jnp.sum(g.astype(F32), axis=0, keepdims=True)
        db_total += jnp.sum(cot_ref[at].astype(F32), axis=0, keepdims=True)
        part[at] = dot(g, up_ref[...], 1, 1)
    ub_out[...] = ub_total
    db_out[...] = db_total
    s0[...] = part[rows_at(rank, own)]
    for r, s in enumerate((s1, s2, s3), 1):
        s[...] = part[rows_at(rank ^ r, own)].astype(BF16)


def quarters_out(meta_ref, total, quarters):
    ctx, bit = meta_ref[1], meta_ref[6]
    size = quarters[0].shape[0]
    own, near, far_near, far_own = quarters
    own[...] = total[rows_at(2 * ctx + bit, size)]
    near[...] = total[rows_at(2 * ctx + 1 - bit, size)]
    far_near[...] = total[rows_at(3 - 2 * ctx - bit, size)]
    far_own[...] = total[rows_at(2 - 2 * ctx + bit, size)]


def quarters_out3(meta_ref, total, quarters):
    own, near, far = quarters
    size = own.shape[0]
    quarters_out(meta_ref, total, (own, near, far.at[:size], far.at[size:]))


def weight_grad_kernel(meta_ref, a_ref, b_ref, *refs):
    total = refs[4]
    total[...] = dot(a_ref[...], b_ref[...], 0, 0).astype(BF16)
    quarters_out(meta_ref, total, refs[:4])


def out_part_kernel(meta_ref, active_ref, down_ref, s0, s2, first, part):
    rank = meta_ref[0]
    own = s0.shape[0]
    part[...] = dot(active_ref[...], down_ref[...], 1, 0)
    s0[...] = part[rows_at(rank, own)]
    s2[...] = part[rows_at(rank ^ 2, own)]
    first[:own] = part[rows_at(rank ^ 1, own)].astype(BF16)
    first[own:] = part[rows_at(rank ^ 3, own)].astype(BF16)


def out_second_kernel(s2, got, out_ref):
    own = s2.shape[0]
    out_ref[...] = (s2[...] + got[own:].astype(F32)).astype(BF16)


def output_kernel(s0, g1, g2, hidden_ref, vec_ref, out_ref):
    own = s0.shape[0]
    total = s0[...] + g1[:own].astype(F32) + g2[...].astype(F32)
    out_ref[...] = (hidden_ref[...] + total + vec(vec_ref, DOWN_BIAS)).astype(BF16)


def sum4(refs):
    total = refs[0][...]
    for ref in refs[1:]:
        total = total + ref[...].astype(F32)
    return total


def norm2_back_kernel(s0, g1, g2, g3, hidden_ref, cot_ref, vec_ref, grad_ref, low_ref, small_ref):
    grad = sum4((s0, g1, g2, g3))
    xhat, scale = norm_parts(hidden_ref[...])
    hidden_grad = cot_ref[...].astype(F32) + norm_back(grad, vec(vec_ref, GAIN2), xhat, scale)
    grad_ref[...] = hidden_grad
    low_ref[...] = hidden_grad.astype(BF16)
    small_ref[0:1] = jnp.sum(grad * xhat, axis=0, keepdims=True)
    small_ref[1:2] = jnp.sum(grad, axis=0, keepdims=True)


def q_back_kernel(
    meta_ref, dq_ref, normed_ref, mix_ref, rows_ref, t0, t1, t2, qb_ref, ob_ref, total
):
    local = dq_ref.shape[0]
    dq = dq_ref[...]
    total[:local] = dot(dq, normed_ref[...], 1, 0).astype(BF16)
    total[local:] = dot(mix_ref[...], rows_ref[...], 1, 0).astype(BF16)
    quarters_out3(meta_ref, total, (t0, t1, t2))
    qb_ref[...] = dot(jnp.ones((8, dq.shape[1]), BF16), dq, 1, 1)[0:1]
    ob_ref[...] = jnp.sum(rows_ref[...].astype(F32), axis=0, keepdims=True)


def kv_back_kernel(
    meta_ref, dq_ref, keep_kv, got_kv, normed_ref, w_ref, x_ref, norm2_ref,
    t0, t1, t2, s0, s2, first, norm_ref, vb_ref, total, part,
):
    rank, ctx = meta_ref[0], meta_ref[1]
    own, width = s0.shape
    half, local = keep_kv.shape[0], keep_kv.shape[1] // 2
    normed = normed_ref[...]
    dkv = (keep_kv[...] + got_kv[rows_at(1 - ctx, half)].astype(F32)).astype(BF16)
    total[...] = dot(dkv, normed, 0, 0).astype(BF16)
    quarters_out3(meta_ref, total, (t0, t1, t2))
    part[...] = dot(dq_ref[...], w_ref[:local], 0, 0) + dot(dkv, w_ref[local:], 1, 0)
    gain_total = jnp.zeros((1, width), F32)
    shift_total = jnp.zeros((1, width), F32)
    chunk = 128
    for c in range(half // chunk):
        at = slice(c * chunk, (c + 1) * chunk)
        xhat, _ = norm_parts(x_ref[at].astype(F32))
        gain_total += jnp.sum(part[at] * xhat, axis=0, keepdims=True)
        shift_total += jnp.sum(part[at], axis=0, keepdims=True)
    norms = jnp.concatenate(
        [gain_total, shift_total, norm2_ref[...], jnp.zeros((4, width), F32)], 0
    )
    norm_ref[...] = norms
    s0[...] = part[rows_at(rank, own)]
    s2[...] = part[rows_at(rank ^ 2, own)]
    first[:own] = part[rows_at(rank ^ 1, own)].astype(BF16)
    first[own : 2 * own] = part[rows_at(rank ^ 3, own)].astype(BF16)
    first[2 * own :] = high_low(norms)
    vb_ref[...] = jnp.sum(dkv.astype(F32), axis=0, keepdims=True)[:, local:]


def rows_second_kernel(s2, got, norm_ref, out_ref, norm_out):
    own = s2.shape[0]
    out_ref[:own] = (s2[...] + got[own : 2 * own].astype(F32)).astype(BF16)
    norms = norm_ref[...] + from_high_low(got[2 * own :])
    norm_out[...] = norms
    out_ref[own:] = high_low(norms)


def last_rows_kernel(
    s0, g1, g2, x_ref, vec1_ref, grad_ref, norm_ref, ob_ref, db_ref, ub_ref, qb_ref, vb_ref, in_out, small_ref
):
    own = s0.shape[0]
    grad = s0[...] + g1[:own].astype(F32) + g2[:own].astype(F32)
    norms = norm_ref[...] + from_high_low(g2[own:])
    xhat, scale = norm_parts(x_ref[...].astype(F32))
    grad = grad_ref[...] + norm_back(grad, vec(vec1_ref, GAIN1), xhat, scale)
    in_out[...] = grad.astype(BF16)
    local = qb_ref.shape[1]
    small_ref[0:4] = norms[:4]
    small_ref[4:5] = ob_ref[...]
    small_ref[5:6] = db_ref[...]
    small_ref[6:7] = ub_ref[...]
    small_ref[7:8] = jnp.zeros_like(ob_ref)
    small_ref[7:8, :local] = qb_ref[...]
    lanes = small_ref.shape[1] // 2
    small_ref[7:8, lanes : lanes + local] = vb_ref[...]


def peer_rows(ctx, pair_ref):
    return pair_ref[rows_at(1 - ctx, pair_ref.shape[0] // 2)]


def place(meta_ref, own_ref, other_ref, own_pair, other_peer, out_ref):
    ctx, bit = meta_ref[1], meta_ref[6]
    size = out_ref.shape[0] // 4
    out_ref[rows_at(2 * ctx + bit, size)] = own_ref[:size].astype(F32)
    out_ref[rows_at(2 * ctx + 1 - bit, size)] = other_ref[:size].astype(F32)
    out_ref[rows_at(2 - 2 * ctx + bit, size)] = peer_rows(ctx, own_pair)[:size].astype(F32)
    other = other_peer if other_peer.shape[0] < 2 * size else peer_rows(ctx, other_peer)
    out_ref[rows_at(3 - 2 * ctx - bit, size)] = other[:size].astype(F32)


def whole_kernel(meta_ref, *refs):
    place(meta_ref, *refs)


def attn_whole_kernel(meta_ref, *refs):
    qkv_out, out_out = refs[8:10]
    total = refs[19]
    local = out_out.shape[0]
    place(meta_ref, *refs[:4], total)
    qkv_out[:local] = total[:local]
    out_out[...] = total[local:]
    place(meta_ref, *refs[4:8], total)
    qkv_out[local:] = total[...]
    rows = total.shape[0] // 4
    tails = [r[rows:] for r in (refs[0], refs[1], refs[3])]
    tails.append(peer_rows(meta_ref[1], refs[2])[rows:])
    small = sum(from_high_low(t) for t in tails)
    outs = refs[10:19]
    for i, out in enumerate(outs[:7]):
        out[...] = small[i]
    lanes = small.shape[1] // 2
    outs[7][...] = small[7, :local]
    outs[8][...] = small[7, lanes : lanes + local]


def to_peers(blocks):
    return [
        lax.ppermute(b, "tensor", xor_pairs(lax.axis_size("tensor"), r))
        for r, b in enumerate(blocks, 1)
    ]


NEAR, FAR = xor_pairs(4, 1), xor_pairs(4, 2)
CTX = xor_pairs(2, 1)


def peer_add_kernel(meta_ref, a_ref, pair_ref, out_ref):
    size = a_ref.shape[0]
    got = pair_ref[rows_at(1 - meta_ref[1], size)].astype(F32)
    out_ref[...] = (a_ref[...].astype(F32) + got).astype(BF16)


def peer_add2_kernel(meta_ref, a_ref, b_ref, pair_ref, a_out, b_out):
    size = a_ref.shape[0]
    peer = 2 - 2 * meta_ref[1]
    a_out[...] = add(a_ref[...], pair_ref[rows_at(peer, size)]).astype(BF16)
    b_out[...] = add(b_ref[...], pair_ref[rows_at(peer + 1, size)]).astype(BF16)


def add(*parts):
    return sum((p.astype(F32) for p in parts[1:]), parts[0].astype(F32))


def high_low(x):
    high = x.astype(BF16).astype(F32)
    return jnp.concatenate([high, x - high], 0).astype(BF16)


def from_high_low(pair):
    pair = pair.astype(F32)
    return pair[:8] + pair[8:]


def sum_kernel(append, tailed, *refs):
    *ins, out_ref = refs
    if append:
        *ins, small_ref = ins
    rows = ins[0].shape[0] - (16 if tailed else 0)
    out_ref[:rows] = add(*(i[:rows] for i in ins)).astype(BF16)
    if append:
        out_ref[rows:] = high_low(small_ref[...])
    if tailed:
        out_ref[rows:] = high_low(sum(from_high_low(i[rows:]) for i in ins))


class Order:
    def __init__(self):
        self.last = None

    def first(self, x):
        return x if self.last is None else after(x, self.last)

    def call(self, kernel, out_shape, args, at=-1, **kw):
        args = list(args)
        args[at] = self.first(args[at])
        out = call(kernel, out_shape, args, **kw)
        self.last = out[0]
        return out

    def step(self, x):
        self.last = self.first(x)
        return self.last

    def pair(self, x):
        self.last = lax.all_gather(self.first(x), "ctx", axis=0, tiled=True)
        return self.last


class WeightSum:
    def __init__(self, order, meta, quarters):
        self.order, self.meta = order, meta
        if len(quarters) == 3:
            self.own, self.near, self.far = quarters
        else:
            self.own, self.near, self.far_near, self.far_own = quarters
        self.shape = [shape(self.own.shape, BF16)]
        self.short = lax.axis_size("dp") == 4

    def both(self):
        got = self.order.pair(self.far)
        send, self.own = self.order.call(
            peer_add2_kernel, self.shape * 2, [self.meta, self.near, self.own, got], smem=1
        )
        self.got = lax.ppermute(send, "dp", NEAR) if self.short else lax.psum(send, "dp")
        self.pair = None

    def one(self):
        got = self.order.pair(self.far_near)
        (send,) = self.order.call(
            peer_add_kernel, self.shape, [self.meta, self.near, got], smem=1
        )
        self.got = lax.ppermute(send, "dp", NEAR) if self.short else lax.psum(send, "dp")

        self.pair = lax.ppermute(self.far_own, "ctx", CTX)

    def three(self, small=None):
        other = self.got if self.short else jnp.zeros_like(self.got)
        args = [self.own, other] + ([] if self.pair is None else [self.pair])
        out = self.shape
        if small is not None:
            rows, cols = self.own.shape
            if not self.short:
                small = lax.psum(small, "dp")
                args = [lax.psum(add(*args).astype(BF16), "dp")]
                self.got = jnp.pad(self.got, ((0, 16), (0, 0)))
            args, out = args + [small], [shape((rows + 16, cols), BF16)]
        kernel = functools.partial(sum_kernel, small is not None, False)
        (self.own,) = self.order.call(kernel, out, args, at=0)
        if self.short:
            self.got = lax.ppermute(self.own, "dp", FAR)
        elif small is None:
            self.own = lax.psum(self.own, "dp")

    def four_add(self):
        if self.short:
            kernel = functools.partial(sum_kernel, False, self.own.shape != self.shape[0].shape)
            out = [shape(self.own.shape, BF16)]
            (self.own,) = self.order.call(kernel, out, [self.own, self.got], at=0)

    def four_send(self):
        if self.short:
            self.got = lax.ppermute(self.own, "dp", NEAR)

    def four(self):
        self.four_add()
        self.four_send()

    def five(self):
        self.own_pair = self.order.pair(self.own)

    def six_now(self):
        self.got_peer = self.order.pair(self.got)

    def six(self):
        self.got_peer = lax.ppermute(self.got, "ctx", CTX)

    def parts(self):
        return [self.own, self.got, self.own_pair, self.got_peer]

    def whole(self):
        rows, cols = self.own.shape
        return self.order.call(
            whole_kernel, [shape((4 * rows, cols), F32)], [self.meta, *self.parts()], smem=1
        )[0]


def per_device(
    tokens,
    lengths,
    norm1_gain,
    norm1_shift,
    qkv_weight,
    query_bias,
    value_bias,
    out_weight,
    out_bias,
    norm2_gain,
    norm2_shift,
    up_weight,
    up_bias,
    down_weight,
    down_bias,
    cotangent,
):
    tokens, cotangent = tokens[0], cotangent[0]
    own, width = tokens.shape
    ranks = lax.axis_size("tensor")
    half = own * ranks
    full = half * lax.axis_size("ctx")
    local = qkv_weight.shape[2]
    hidden_units = up_weight.shape[1]
    rank = lax.axis_index("tensor")
    ctx = lax.axis_index("ctx")
    bit = lax.axis_index("dp") & 1
    meta = jnp.concatenate(
        [jnp.stack([rank, ctx]).astype(jnp.int32), lengths[0], bit.astype(jnp.int32)[None]]
    )
    weight_t = jnp.transpose(qkv_weight, (1, 2, 0)).reshape(3 * local, width)
    size = 128
    block = shape((own, width), F32)
    block_low = shape((own, width), BF16)
    row_out = shape((1, width), F32)

    def quarters(rows_all, cols):
        return [shape((rows_all // 4, cols), BF16)] * 4

    def quarters3(rows_all, cols):
        return quarters(rows_all, cols)[:2] + [shape((rows_all // 2, cols), BF16)]

    order = Order()
    xs = to_peers([tokens] * 3)
    vectors1, weight_t, own_x, message = call(
        first_kernel,
        [
            shape((8, width), F32),
            shape(weight_t.shape, BF16),
            block_low,
            shape((own + local // 2, width), BF16),
        ],
        [meta, norm1_gain, norm1_shift, query_bias, value_bias]
        + [weight_t, tokens, cotangent, out_weight],
        smem=1,
    )
    rows, normed1, q, kv = order.call(
        qkv_kernel,
        [shape((half, width), BF16)] * 2
        + [shape((half, local), BF16), shape((half, 2 * local), BF16)],
        [meta, own_x, *xs, vectors1, weight_t],
        smem=1,
    )
    cots = to_peers([after(message, *xs)] * 3)
    kv_all = order.pair(kv)
    mix, lse = order.call(
        functools.partial(attend_kernel, size),
        [shape((local, half), BF16), shape((8, half), F32)],
        [meta, q, kv_all],
        smem=1,
        scratch=[pltpu.VMEM((full, local), BF16), pltpu.VMEM((local, full), BF16)],
    )
    mixes = to_peers([mix] * 3)
    pieces = jnp.concatenate([after(cots[0], mix)[own:], cots[1][own:], cots[2][own:]], 0)
    pieces_ctx = order.pair(pieces)
    (vectors,) = order.call(
        pack_kernel,
        [shape((8, width), F32)],
        [out_bias, norm2_gain, norm2_shift, up_bias, down_bias],
    )
    (normed2, active, up_grad, cot_rows, hidden, *normed2_parts, up_bias_part, down_bias_part) = order.call(
        ff_kernel,
        [
            shape((half, width), BF16),
            shape((half, hidden_units), BF16),
            shape((half, hidden_units), BF16),
            shape((half, width), BF16),
            block,
            block,
            block_low,
            block_low,
            block_low,
            shape((1, hidden_units), F32),
            row_out,
        ],
        [meta, mix, *mixes, rows, out_weight, pieces_ctx, vectors]
        + [up_weight, down_weight, cotangent, *cots],
        smem=1,
        vmem=28,
        scratch=[
            pltpu.VMEM((ranks * local, width), BF16),
            pltpu.VMEM((ranks * local, half), BF16),
            pltpu.VMEM((half, width), F32),
        ],
    )
    normed2_got = to_peers(normed2_parts[1:])

    def weight_grad(a, b):
        rows_all, cols = a.shape[1], b.shape[1]
        out = order.call(
            weight_grad_kernel,
            quarters(rows_all, cols),
            [meta, a, b],
            smem=1,
            scratch=[pltpu.VMEM((rows_all, cols), BF16)],
        )
        return WeightSum(order, meta, out)

    down_sum = weight_grad(active, cot_rows)
    down_sum.one()
    up_sum = weight_grad(normed2, up_grad)
    hidden_grad, branch_grad, norm2_part = order.call(
        norm2_back_kernel,
        [block, block_low, shape((2, width), F32)],
        [normed2_parts[0], *normed2_got, hidden, cotangent, vectors],
        at=0,
    )
    branches = to_peers([branch_grad] * 3)
    up_sum.one()
    down_sum.three()
    o0, o2, o_first = order.call(
        out_part_kernel,
        [block, block, shape((2 * own, width), BF16)],
        [meta, active, down_weight],
        at=1,
        smem=1,
        scratch=[pltpu.VMEM((half, width), F32)],
    )
    dq, kv_keep, kv_send, branch_rows = order.call(
        functools.partial(back_kernel, size),
        [
            shape((local, half), BF16),
            shape((half, 2 * local), F32),
            shape((half, 2 * local), BF16),
            shape((half, width), BF16),
        ],
        [meta, q, kv_all, lse, branch_grad, *branches, out_weight],
        at=1,
        smem=1,
        vmem=24,
        scratch=[
            pltpu.VMEM((full, local), BF16),
            pltpu.VMEM((local, full), BF16),
            pltpu.VMEM((full, local), BF16),
            pltpu.VMEM((half, local), BF16),
            pltpu.VMEM((full, local), F32),
            pltpu.VMEM((full, local), F32),
            pltpu.VMEM((full, local // HEAD_DIM * size), BF16),
            pltpu.VMEM((full, local // HEAD_DIM * size), BF16),
        ],
    )
    kv_got = order.pair(kv_send)
    up_sum.three()
    down_sum.four_add()
    x_pairs, y_pairs = xor_pairs(ranks, 1), xor_pairs(ranks, 2)
    *kv_quarters, n0, n2, n_first, norm_part, v_bias_part = order.call(
        kv_back_kernel,
        quarters3(2 * local, width)
        + [block, block, shape((2 * own + 16, width), BF16)]
        + [shape((8, width), F32), shape((1, local), F32)],
        [meta, dq, kv_keep, kv_got, normed1, weight_t, rows, norm2_part],
        at=1,
        smem=1,
        scratch=[pltpu.VMEM((2 * local, width), BF16), pltpu.VMEM((half, width), F32)],
    )
    n_first_got = lax.ppermute(n_first, "tensor", x_pairs)
    kv_sum = WeightSum(order, meta, kv_quarters)
    kv_sum.both()
    *qo_quarters, q_bias_part, out_bias_part = order.call(
        q_back_kernel,
        quarters3(2 * local, width) + [shape((1, local), F32), row_out],
        [meta, dq, normed1, mix, branch_rows],
        at=1,
        smem=1,
        scratch=[pltpu.VMEM((2 * local, width), BF16)],
    )
    qo_sum = WeightSum(order, meta, qo_quarters)
    qo_sum.both()
    n_second, norm_part = order.call(
        rows_second_kernel,
        [shape((own + 16, width), BF16), shape((8, width), F32)],
        [n2, n_first_got, norm_part],
        at=0,
    )
    n_second_got = lax.ppermute(n_second, "tensor", y_pairs)
    kv_sum.three()
    up_sum.four_add()
    input_grad, small = order.call(
        last_rows_kernel,
        [block_low, shape((8, width), F32)],
        [n0, n_first_got, n_second_got, own_x, vectors1, hidden_grad, norm_part]
        + [out_bias_part, down_bias_part, up_bias_part, q_bias_part, v_bias_part],
        at=0,
    )
    qo_sum.three(small)
    down_sum.own = after(down_sum.own, qo_sum.own)
    down_sum.four_send()
    up_sum.own = after(up_sum.own, qo_sum.own)
    up_sum.four_send()
    o_first_got = lax.ppermute(after(o_first, small), "tensor", x_pairs)
    down_sum.five()
    up_sum.five()
    (o_second,) = order.call(out_second_kernel, [block_low], [o2, o_first_got], at=0)
    o_second_got = lax.ppermute(o_second, "tensor", y_pairs)
    down_sum.got = order.step(down_sum.got)
    down_sum.six_now()
    down_grad = down_sum.whole()
    up_sum.got = order.step(up_sum.got)
    kv_sum.four()
    qo_sum.four()
    kv_sum.five()
    qo_sum.five()
    up_sum.six()
    up_weight_grad = up_sum.whole()
    kv_sum.got = order.step(kv_sum.got)
    qo_sum.got = order.step(qo_sum.got)
    (output,) = order.call(
        output_kernel, [block_low], [o0, o_first_got, o_second_got, hidden, vectors], at=0
    )
    kv_sum.six()
    qo_sum.six()
    attn_grad, out_weight_grad, *outs = order.call(
        attn_whole_kernel,
        [shape((3 * local, width), F32), shape((local, width), F32)]
        + [shape((width,), F32)] * 7
        + [shape((local,), F32)] * 2,
        [meta, *qo_sum.parts(), *kv_sum.parts()],
        smem=1,
        scratch=[pltpu.VMEM((2 * local, width), F32)],
    )
    n1g, n1s, n2g, n2s, out_bias_grad, down_bias_grad, up_bias_grad, q_bias_grad, v_bias_grad = outs
    return (
        output[None],
        input_grad[None],
        n1g,
        n1s,
        jnp.transpose(attn_grad.reshape(3, local, width), (2, 0, 1)),
        q_bias_grad,
        v_bias_grad,
        out_weight_grad,
        out_bias_grad,
        n2g,
        n2s,
        up_weight_grad,
        up_bias_grad,
        down_grad,
        down_bias_grad,
    )


def solution(mesh):
    row_spec = P("dp", ("ctx", "tensor"), None)
    return jax.shard_map(
        per_device,
        mesh=mesh,
        in_specs=(
            row_spec,
            P("dp", None),
            P(),
            P(),
            P(None, None, "tensor"),
            P("tensor"),
            P("tensor"),
            P("tensor", None),
            P(),
            P(),
            P(),
            P(None, "tensor"),
            P("tensor"),
            P("tensor", None),
            P(),
            row_spec,
        ),
        out_specs=(
            row_spec,
            row_spec,
            P(),
            P(),
            P(None, None, "tensor"),
            P("tensor"),
            P("tensor"),
            P("tensor", None),
            P(),
            P(),
            P(),
            P(None, "tensor"),
            P("tensor"),
            P("tensor", None),
            P(),
        ),
        check_vma=False,
    )
```
